512 devices in a mesh: rep: 8 (over z_hi, core), row: 8 (over z_lo, x), col: 8 (over y).
Axes of the slice: x: 4, y: 8, z: 8 (z_hi: 4, z_lo: 2; z = z_hi * 2 + z_lo), core: 2. Of those that a mesh axis runs over, the one named last changes fastest.
Arguments:
- inputs: bfloat16 [8, 128, 6144], P('rep', 'col', 'row'), may hold values from -6 to 6
- w_in: bfloat16 [6144, 24576], P('row', ('rep', 'col')), may hold values from -0.078125 to 0.078125
- w_out: bfloat16 [24576, 6144], P(('rep', 'col'), 'row'), may hold values from -0.0390625 to 0.0390625
- cotangent: bfloat16 [8, 128, 6144], P('rep', 'col', 'row'), may hold values from -3072 to 3072
- counts: int32 [8], replicated, may hold values from 0 to 4, as said below
Outputs:
- block_output: bfloat16 [8, 128, 6144], P('rep', 'col', 'row')
- input_grad: bfloat16 [8, 128, 6144], P('rep', 'col', 'row')
- w_in_grad: float32 [6144, 24576], P('row', ('rep', 'col'))
- w_out_grad: float32 [24576, 6144], P(('rep', 'col'), 'row')
The draws below stay inside these ranges and needn't reach their ends.
Inputs may be any that keep to these rules, and one draw needn't show every extreme that they name: Replica r completed its first counts[r] micro-batches; at least one replica completed all 4.
All inputs are finite; a program needn't handle non-finite values.
Results may differ from the reference program's by a relative error of at most 0.015.
Values may be sent and summed in bfloat16 or wider, within the bound.
No kernel may reach another device: no remote copies, remote signals or barrier semaphores. Data moves between devices by JAX's collectives and lax.ppermute only.
A program may use at most 64 MiB of HBM per device.

```python
import jax
import jax.numpy as jnp

D = 6144
FF = 24576
MB = 4
MBT = 32
TOKENS = 128
N_REP = 8
N_ROW = 8
N_COL = 8


def draw_counts(key, part):
    first = jax.random.fold_in(key, 11)
    second = jax.random.fold_in(key, 23)
    values = jax.random.randint(first, (N_REP,), 0, MB + 1)
    chosen = jax.random.randint(second, (), 0, N_REP)
    return jnp.where(jnp.arange(N_REP) == chosen, MB, values).astype(jnp.int32)


def block_scale(stream_key, dims, cuts, least, top_value):
    level, own = 1.0, jax.random.fold_in(stream_key, 6)
    for axis_at, blocks in cuts:
        steps = jnp.exp(jax.random.uniform(jax.random.fold_in(own, axis_at), (blocks,), jnp.float32, least / len(cuts), top_value / len(cuts)))
        level = level * jnp.repeat(steps, dims[axis_at] // blocks).reshape([-1 if axis == axis_at else 1 for axis in range(len(dims))])
    return level


def noise(rng, dims, spread, most, shards=(), held_as=jnp.bfloat16):
    array = jax.random.normal(rng, dims, jnp.float32) * spread
    if len(shards) > 0:
        array = block_scale(rng, dims, shards, -0.22, 0.18) * array
    return jnp.clip(array, min=-most, max=most).astype(held_as)


def setup_inputs(seed: int = 0) -> dict:
    streams_of = jax.random.split(jax.random.key(seed), 6)
    return {
        "inputs": noise(streams_of[0], (N_REP, TOKENS, D), 1.0, 6.0, ((0, 8), (1, 8), (2, 8))),
        "w_in": noise(streams_of[1], (D, FF), D ** -0.5, 0.078125, ((0, 8), (1, 64))),
        "w_out": noise(streams_of[2], (FF, D), FF ** -0.5, 0.0390625, ((0, 64), (1, 8))),
        "cotangent": noise(streams_of[3], (N_REP, TOKENS, D), (MBT * MB * N_REP // 2), 3072.0, ((0, 8), (1, 8), (2, 8))),
        "counts": draw_counts(jax.random.fold_in(streams_of[5], 71), 0),
    }


root_coef = 0.7978845608028654
cubic_coef = 0.044715


def gelu_tanh(values):
    inner = root_coef * (values + cubic_coef * values * values * values)
    return 0.5 * values * (1.0 + jnp.tanh(inner))


def gelu_slope(values):
    inner = root_coef * (values + cubic_coef * values * values * values)
    tangent = jnp.tanh(inner)
    return 0.5 * (1.0 + tangent) + 0.5 * values * (1.0 - tangent * tangent) * root_coef * (1.0 + 3.0 * cubic_coef * values * values)


def rounded_term(left, right):
    return jnp.dot(left, right, preferred_element_type=jnp.float32).astype(jnp.bfloat16).astype(jnp.float32)


def block_sum(left, right):
    width = left.shape[1] // N_ROW
    total = jnp.zeros((left.shape[0], right.shape[1]), jnp.float32)
    for block in range(N_ROW):
        total = total + rounded_term(left[:, block * width:(block + 1) * width], right[block * width:(block + 1) * width, :])
    return total


def set_sum(left, right):
    piece = FF // (N_REP * N_COL)
    left_sets = left.reshape(left.shape[0], N_REP, N_COL, piece)
    right_sets = right.reshape(N_REP, N_COL, piece, right.shape[1])
    total = jnp.zeros((left.shape[0], right.shape[1]), jnp.float32)
    for group in range(N_COL):
        left_part = left_sets[:, :, group, :].reshape(left.shape[0], N_REP * piece)
        right_part = right_sets[:, group, :, :].reshape(N_REP * piece, right.shape[1])
        total = total + rounded_term(left_part, right_part)
    return total


def reference(inputs, w_in, w_out, cotangent, counts):
    token_total = (MBT * jnp.sum(counts)).astype(jnp.float32)
    positions = jnp.arange(MB * MBT, dtype=jnp.int32)
    outputs = []
    grads = []
    w_in_grad = jnp.zeros((D, FF), jnp.float32)
    w_out_grad = jnp.zeros((FF, D), jnp.float32)
    w_out_t = w_out.T
    w_in_t = w_in.T
    for replica in range(N_REP):
        tokens = inputs[replica]
        kept_mask = (positions // MBT < counts[replica]).astype(jnp.float32)
        hidden = block_sum(tokens, w_in)
        activated = gelu_tanh(hidden).astype(jnp.bfloat16)
        mixed = set_sum(activated, w_out)
        outputs.append((tokens.astype(jnp.float32) + mixed).astype(jnp.bfloat16))
        scaled = (cotangent[replica].astype(jnp.float32) * kept_mask[:, None] / token_total).astype(jnp.bfloat16)
        slope_sum = block_sum(scaled, w_out_t)
        hidden_grad = (slope_sum * gelu_slope(hidden)).astype(jnp.bfloat16)
        back = set_sum(hidden_grad, w_in_t)
        grads.append((scaled.astype(jnp.float32) + back).astype(jnp.bfloat16))
        w_in_grad = w_in_grad + jnp.dot(tokens.T, hidden_grad, preferred_element_type=jnp.float32)
        w_out_grad = w_out_grad + jnp.dot(activated.T, scaled, preferred_element_type=jnp.float32)
    return (jnp.stack(outputs), jnp.stack(grads), w_in_grad, w_out_grad)
```

```python
import jax
import jax.numpy as jnp
from jax import lax
from jax.sharding import PartitionSpec as P

MBT = 32


root_coef = 0.7978845608028654
cubic_coef = 0.044715


def gelu_both(values):
    inner = root_coef * (values + cubic_coef * values * values * values)
    tangent = jnp.tanh(inner)
    slope = 0.5 * (1.0 + tangent) + 0.5 * values * (1.0 - tangent * tangent) * root_coef * (
        1.0 + 3.0 * cubic_coef * values * values
    )
    return 0.5 * values * (1.0 + tangent), slope


def product(left, right, left_dim, right_dim):
    return lax.dot_general(
        left, right, (((left_dim,), (right_dim,)), ((), ())), preferred_element_type=jnp.float32
    )


def summed_on_arrival(value, axis):
    size = lax.axis_size(axis)
    rows, width = value.shape
    pieces = lax.all_to_all(value.reshape(size, rows // size, width), axis, 0, 0, tiled=True)
    return jnp.sum(pieces.astype(jnp.float32), axis=0)


def body(inputs, w_in, w_out, cotangent, counts):
    rows_local = inputs.shape[1]
    width = inputs.shape[2]
    units = w_in.shape[1]
    tokens_local = inputs.reshape(rows_local, width)
    replicas = lax.axis_size("rep")
    columns = lax.axis_size("col")
    replica_index = lax.axis_index("rep")
    column_index = lax.axis_index("col")
    own_count = jnp.sum(jnp.where(jnp.arange(replicas) == replica_index, counts, 0))
    token_total = (MBT * jnp.sum(counts)).astype(jnp.float32)
    positions = column_index * rows_local + jnp.arange(rows_local, dtype=jnp.int32)
    kept_mask = (positions // MBT < own_count).astype(jnp.float32)
    scaled = (
        cotangent.reshape(rows_local, width).astype(jnp.float32)
        * kept_mask[:, None]
        / token_total
    ).astype(jnp.bfloat16)
    both = jnp.concatenate([tokens_local, scaled], axis=1)
    everyone = lax.all_gather(both, ("rep", "col"), axis=0, tiled=True)
    tokens_all, scaled_all = everyone[:, :width], everyone[:, width:]
    hidden_terms = product(tokens_all, w_in, 1, 0).astype(jnp.bfloat16)
    slope_terms = product(scaled_all, w_out, 1, 1).astype(jnp.bfloat16)
    sums = summed_on_arrival(jnp.concatenate([hidden_terms, slope_terms], axis=1), "row")
    active, slope = gelu_both(sums[:, :units])
    active_share = active.astype(jnp.bfloat16)
    grad_share = (sums[:, units:] * slope).astype(jnp.bfloat16)
    shares = lax.all_gather(
        jnp.concatenate([active_share, grad_share], axis=1), "row", axis=0, tiled=True
    )
    activated, hidden_grad = shares[:, :units], shares[:, units:]
    output_terms = product(activated, w_out, 1, 0).astype(jnp.bfloat16)
    back_terms = product(hidden_grad, w_in, 1, 1).astype(jnp.bfloat16)
    terms = jnp.concatenate([output_terms, back_terms], axis=1)
    by_rep = summed_on_arrival(terms, "rep").astype(jnp.bfloat16)
    finished = summed_on_arrival(by_rep, "col")
    block_output = (tokens_local.astype(jnp.float32) + finished[:, :width]).astype(jnp.bfloat16)
    input_grad = (scaled.astype(jnp.float32) + finished[:, width:]).astype(jnp.bfloat16)
    w_in_grad = product(tokens_all, hidden_grad, 0, 0)
    w_out_grad = product(activated, scaled_all, 0, 0)
    return (
        block_output.reshape(1, rows_local, width),
        input_grad.reshape(1, rows_local, width),
        w_in_grad,
        w_out_grad,
    )


def solution(mesh):
    placed = (
        P("rep", "col", "row"),
        P("row", ("rep", "col")),
        P(("rep", "col"), "row"),
        P("rep", "col", "row"),
        P(),
    )
    return jax.shard_map(
        body,
        mesh=mesh,
        in_specs=placed,
        out_specs=(
            P("rep", "col", "row"),
            P("rep", "col", "row"),
            P("row", ("rep", "col")),
            P(("rep", "col"), "row"),
        ),
        check_vma=False,
    )
```

```python
import jax
import jax.numpy as jnp
from jax import lax
from jax.sharding import PartitionSpec as P

MBT = 32
CORES = 2

root_coef = 0.7978845608028654
cubic_coef = 0.044715


def gelu_both(values):
    inner = root_coef * (values + cubic_coef * values * values * values)
    tangent = jnp.tanh(inner)
    slope = 0.5 * (1.0 + tangent) + 0.5 * values * (1.0 - tangent * tangent) * root_coef * (
        1.0 + 3.0 * cubic_coef * values * values
    )
    return 0.5 * values * (1.0 + tangent), slope


def product(left, right, left_dim, right_dim):
    return lax.dot_general(
        left, right, (((left_dim,), (right_dim,)), ((), ())), preferred_element_type=jnp.float32
    )


def cut(value, pieces):
    rows, width = value.shape
    return value.reshape(pieces, rows // pieces, width)


def swapped(value, axis, groups=None):
    return lax.all_to_all(value, axis, 0, 0, axis_index_groups=groups, tiled=True)


def added_up(pieces):
    total = pieces[0].astype(jnp.float32)
    for at in range(1, pieces.shape[0]):
        total = total + pieces[at].astype(jnp.float32)
    return total


def spread(value, axis, size, groups=None):
    return swapped(jnp.broadcast_to(value[None], (size, *value.shape)), axis, groups)


def body(inputs, w_in, w_out, cotangent, counts):
    rows_local = inputs.shape[1]
    width = inputs.shape[2]
    units = w_in.shape[1]
    replicas = lax.axis_size("rep")
    columns = lax.axis_size("col")
    row_count = lax.axis_size("row")
    chips = replicas // CORES
    same_core = [[chip * CORES + core for chip in range(chips)] for core in range(CORES)]
    to_mate = [(r, r // CORES * CORES + (r + 1) % CORES) for r in range(replicas)]
    mate = lambda value: lax.ppermute(value, "rep", to_mate)

    tokens_local = inputs.reshape(rows_local, width)
    replica_index = lax.axis_index("rep")
    column_index = lax.axis_index("col")
    own_count = jnp.sum(jnp.where(jnp.arange(replicas) == replica_index, counts, 0))
    token_total = (MBT * jnp.sum(counts)).astype(jnp.float32)
    positions = column_index * rows_local + jnp.arange(rows_local, dtype=jnp.int32)
    kept_mask = (positions // MBT < own_count).astype(jnp.float32)
    scaled = (
        cotangent.reshape(rows_local, width).astype(jnp.float32)
        * kept_mask[:, None]
        / token_total
    ).astype(jnp.bfloat16)

    w_in_mate, w_out_mate = mate(w_in), mate(w_out)

    line = spread(jnp.concatenate([tokens_local, scaled], axis=0), "rep", chips, same_core)
    tokens_line = line[:, :rows_local].reshape(chips * rows_local, width)
    scaled_line = line[:, rows_local:].reshape(chips * rows_local, width)
    line_rows = chips * rows_local
    rows_all = columns * line_rows

    padded = jnp.concatenate([scaled_line, scaled_line[: line_rows // 2]], axis=0)
    scaled_all = lax.all_gather(padded, "col", axis=0)[:, :line_rows].reshape(rows_all, width)

    tokens_all = spread(tokens_line, "col", columns).reshape(rows_all, width)
    hidden_terms = jnp.concatenate(
        [product(tokens_all, w, 1, 0).astype(jnp.bfloat16) for w in (w_in, w_in_mate)], axis=1
    )
    hidden = added_up(swapped(cut(hidden_terms, row_count), "row"))
    active, slope = gelu_both(hidden)
    active, scaled_all = lax.optimization_barrier((active, scaled_all))
    activated = spread(active.astype(jnp.bfloat16), "row", row_count).reshape(rows_all, -1)

    slope_terms = jnp.concatenate(
        [product(scaled_all, w, 1, 1).astype(jnp.bfloat16) for w in (w_out, w_out_mate)], axis=1
    )
    slope_terms, activated = lax.optimization_barrier((slope_terms, activated))
    slope_sum = added_up(swapped(cut(slope_terms, row_count), "row"))
    grad_share = (slope_sum * slope).astype(jnp.bfloat16)

    output_terms = (
        product(activated[:, :units], w_out, 1, 0) + product(activated[:, units:], w_out_mate, 1, 0)
    ).astype(jnp.bfloat16)
    grad_share, output_terms = lax.optimization_barrier((grad_share, output_terms))
    hidden_grad = spread(grad_share, "row", row_count).reshape(rows_all, -1)
    output_line = lax.psum_scatter(output_terms, "col", scatter_dimension=0, tiled=True)

    back_terms = (
        product(hidden_grad[:, :units], w_in, 1, 1) + product(hidden_grad[:, units:], w_in_mate, 1, 1)
    ).astype(jnp.bfloat16)
    back_line = added_up(swapped(cut(back_terms, columns), "col")).astype(jnp.bfloat16)

    ends = jnp.concatenate([cut(output_line, chips), cut(back_line, chips)], axis=1)
    finished = added_up(swapped(ends, "rep", same_core))
    block_output = (tokens_local.astype(jnp.float32) + finished[:rows_local]).astype(jnp.bfloat16)
    input_grad = (scaled.astype(jnp.float32) + finished[rows_local:]).astype(jnp.bfloat16)

    tokens_mate, scaled_mate = mate(tokens_all), mate(scaled_all)
    active_mate, grad_mate = mate(activated[:, units:]), mate(hidden_grad[:, units:])
    w_in_grad = product(tokens_all, hidden_grad[:, :units], 0, 0) + product(
        tokens_mate, grad_mate, 0, 0
    )
    w_out_grad = product(activated[:, :units], scaled_all, 0, 0) + product(
        active_mate, scaled_mate, 0, 0
    )
    return (
        block_output.reshape(1, rows_local, width),
        input_grad.reshape(1, rows_local, width),
        w_in_grad,
        w_out_grad,
    )


def solution(mesh):
    placed = (
        P("rep", "col", "row"),
        P("row", ("rep", "col")),
        P(("rep", "col"), "row"),
        P("rep", "col", "row"),
        P(),
    )
    return jax.shard_map(
        body,
        mesh=mesh,
        in_specs=placed,
        out_specs=(
            P("rep", "col", "row"),
            P("rep", "col", "row"),
            P("row", ("rep", "col")),
            P(("rep", "col"), "row"),
        ),
        check_vma=False,
    )
```

```python
import jax
import jax.numpy as jnp
from jax import lax
from jax.sharding import PartitionSpec as P

MBT = 32
CORES = 2

root_coef = 0.7978845608028654
cubic_coef = 0.044715


def gelu_both(values):
    inner = root_coef * (values + cubic_coef * values * values * values)
    tangent = jnp.tanh(inner)
    slope = 0.5 * (1.0 + tangent) + 0.5 * values * (1.0 - tangent * tangent) * root_coef * (
        1.0 + 3.0 * cubic_coef * values * values
    )
    return 0.5 * values * (1.0 + tangent), slope


def product(left, right, left_dim, right_dim):
    return lax.dot_general(
        left, right, (((left_dim,), (right_dim,)), ((), ())), preferred_element_type=jnp.float32
    )


def cut(value, pieces):
    rows, width = value.shape
    return value.reshape(pieces, rows // pieces, width)


def swapped(value, axis, groups=None):
    return lax.all_to_all(value, axis, 0, 0, axis_index_groups=groups, tiled=True)


def added_up(pieces):
    total = pieces[0].astype(jnp.float32)
    for at in range(1, pieces.shape[0]):
        total = total + pieces[at].astype(jnp.float32)
    return total


def spread(value, axis, size, groups=None):
    return swapped(jnp.broadcast_to(value[None], (size, *value.shape)), axis, groups)


def body(inputs, w_in, w_out, cotangent, counts):
    rows_local = inputs.shape[1]
    width = inputs.shape[2]
    units = w_in.shape[1]
    replicas = lax.axis_size("rep")
    columns = lax.axis_size("col")
    row_count = lax.axis_size("row")
    chips = replicas // CORES
    same_core = [[chip * CORES + core for chip in range(chips)] for core in range(CORES)]
    to_mate = [(r, r // CORES * CORES + (r + 1) % CORES) for r in range(replicas)]
    mate = lambda value: lax.ppermute(value, "rep", to_mate)

    tokens_local = inputs.reshape(rows_local, width)
    replica_index = lax.axis_index("rep")
    column_index = lax.axis_index("col")
    own_count = jnp.sum(jnp.where(jnp.arange(replicas) == replica_index, counts, 0))
    token_total = (MBT * jnp.sum(counts)).astype(jnp.float32)
    positions = column_index * rows_local + jnp.arange(rows_local, dtype=jnp.int32)
    kept_mask = (positions // MBT < own_count).astype(jnp.float32)
    scaled = (
        cotangent.reshape(rows_local, width).astype(jnp.float32)
        * kept_mask[:, None]
        / token_total
    ).astype(jnp.bfloat16)

    w_in_mate, w_out_mate = mate(w_in), mate(w_out)

    line = spread(jnp.concatenate([tokens_local, scaled], axis=0), "rep", chips, same_core)
    tokens_line = line[:, :rows_local].reshape(chips * rows_local, width)
    scaled_line = line[:, rows_local:].reshape(chips * rows_local, width)
    line_rows = chips * rows_local
    rows_all = columns * line_rows

    padded = jnp.concatenate([scaled_line, scaled_line[: line_rows // 2]], axis=0)
    scaled_all = lax.all_gather(padded, "col", axis=0)[:, :line_rows].reshape(rows_all, width)

    tokens_all = spread(tokens_line, "col", columns).reshape(rows_all, width)
    hidden_terms = jnp.concatenate(
        [product(tokens_all, w, 1, 0).astype(jnp.bfloat16) for w in (w_in, w_in_mate)], axis=1
    )
    hidden = added_up(swapped(cut(hidden_terms, row_count), "row"))
    active, slope = gelu_both(hidden)
    active, scaled_all = lax.optimization_barrier((active, scaled_all))
    activated = spread(active.astype(jnp.bfloat16), "row", row_count).reshape(rows_all, -1)

    slope_terms = jnp.concatenate(
        [product(scaled_all, w, 1, 1).astype(jnp.bfloat16) for w in (w_out, w_out_mate)], axis=1
    )
    slope_terms, activated = lax.optimization_barrier((slope_terms, activated))
    slope_sum = added_up(swapped(cut(slope_terms, row_count), "row"))
    grad_share = (slope_sum * slope).astype(jnp.bfloat16)

    output_terms = (
        product(activated[:, :units], w_out, 1, 0) + product(activated[:, units:], w_out_mate, 1, 0)
    ).astype(jnp.bfloat16)
    grad_share, output_terms = lax.optimization_barrier((grad_share, output_terms))
    hidden_grad = spread(grad_share, "row", row_count).reshape(rows_all, -1)
    output_line = lax.psum_scatter(output_terms, "col", scatter_dimension=0, tiled=True)

    back_terms = (
        product(hidden_grad[:, :units], w_in, 1, 1) + product(hidden_grad[:, units:], w_in_mate, 1, 1)
    ).astype(jnp.bfloat16)
    back_line = added_up(swapped(cut(back_terms, columns), "col")).astype(jnp.bfloat16)

    hidden_grad, scaled_all, output_line = lax.optimization_barrier((hidden_grad, scaled_all, output_line))
    w_out_grad = product(activated[:, :units], scaled_all, 0, 0) + product(
        mate(activated[:, units:]), mate(scaled_all), 0, 0
    )

    w_in_grad = product(tokens_all, hidden_grad[:, :units], 0, 0) + product(
        mate(tokens_all), mate(hidden_grad[:, units:]), 0, 0
    )
    ends = jnp.concatenate([cut(output_line, chips), cut(back_line, chips)], axis=1)
    finished = added_up(swapped(ends, "rep", same_core))
    block_output = (tokens_local.astype(jnp.float32) + finished[:rows_local]).astype(jnp.bfloat16)
    input_grad = (scaled.astype(jnp.float32) + finished[rows_local:]).astype(jnp.bfloat16)

    return (
        block_output.reshape(1, rows_local, width),
        input_grad.reshape(1, rows_local, width),
        w_in_grad,
        w_out_grad,
    )


def solution(mesh):
    placed = (
        P("rep", "col", "row"),
        P("row", ("rep", "col")),
        P(("rep", "col"), "row"),
        P("rep", "col", "row"),
        P(),
    )
    return jax.shard_map(
        body,
        mesh=mesh,
        in_specs=placed,
        out_specs=(
            P("rep", "col", "row"),
            P("rep", "col", "row"),
            P("row", ("rep", "col")),
            P(("rep", "col"), "row"),
        ),
        check_vma=False,
    )
```

```python
import jax
import jax.numpy as jnp
from jax import lax
from jax.sharding import PartitionSpec as P

MBT = 32
CORES = 2

root_coef = 0.7978845608028654
cubic_coef = 0.044715


def gelu_both(values):
    inner = root_coef * (values + cubic_coef * values * values * values)
    tangent = jnp.tanh(inner)
    slope = 0.5 * (1.0 + tangent) + 0.5 * values * (1.0 - tangent * tangent) * root_coef * (
        1.0 + 3.0 * cubic_coef * values * values
    )
    return 0.5 * values * (1.0 + tangent), slope


def product(left, right, left_dim, right_dim):
    return lax.dot_general(
        left, right, (((left_dim,), (right_dim,)), ((), ())), preferred_element_type=jnp.float32
    )


def cut(value, pieces):
    rows, width = value.shape
    return value.reshape(pieces, rows // pieces, width)


def swapped(value, axis, groups=None):
    return lax.all_to_all(value, axis, 0, 0, axis_index_groups=groups, tiled=True)


def added_up(pieces):
    total = pieces[0].astype(jnp.float32)
    for at in range(1, pieces.shape[0]):
        total = total + pieces[at].astype(jnp.float32)
    return total


def spread(value, axis, size, groups=None):
    return swapped(jnp.broadcast_to(value[None], (size, *value.shape)), axis, groups)


def body(inputs, w_in, w_out, cotangent, counts):
    rows_local = inputs.shape[1]
    width = inputs.shape[2]
    units = w_in.shape[1]
    replicas = lax.axis_size("rep")
    columns = lax.axis_size("col")
    row_count = lax.axis_size("row")
    chips = replicas // CORES
    same_core = [[chip * CORES + core for chip in range(chips)] for core in range(CORES)]
    to_mate = [(r, r // CORES * CORES + (r + 1) % CORES) for r in range(replicas)]
    mate = lambda value: lax.ppermute(value, "rep", to_mate)

    tokens_local = inputs.reshape(rows_local, width)
    replica_index = lax.axis_index("rep")
    column_index = lax.axis_index("col")
    own_count = jnp.sum(jnp.where(jnp.arange(replicas) == replica_index, counts, 0))
    token_total = (MBT * jnp.sum(counts)).astype(jnp.float32)
    positions = column_index * rows_local + jnp.arange(rows_local, dtype=jnp.int32)
    kept_mask = (positions // MBT < own_count).astype(jnp.float32)
    scaled = (
        cotangent.reshape(rows_local, width).astype(jnp.float32)
        * kept_mask[:, None]
        / token_total
    ).astype(jnp.bfloat16)

    w_in_mate, w_out_mate = mate(w_in), mate(w_out)

    line = spread(jnp.concatenate([tokens_local, scaled], axis=0), "rep", chips, same_core)
    tokens_line = line[:, :rows_local].reshape(chips * rows_local, width)
    scaled_line = line[:, rows_local:].reshape(chips * rows_local, width)
    line_rows = chips * rows_local
    rows_all = columns * line_rows

    padded = jnp.concatenate([scaled_line, scaled_line[: line_rows // 2]], axis=0)
    scaled_all = lax.all_gather(padded, "col", axis=0)[:, :line_rows].reshape(rows_all, width)

    def forward(line):
        everyone = spread(line, "col", columns).reshape(rows_all, width)
        return everyone, hidden_part(everyone)

    def forward_plain(line):
        everyone = lax.all_gather(line, "col", axis=0, tiled=True)
        return everyone, hidden_part(everyone)

    def hidden_part(everyone):
        return jnp.concatenate(
            [product(everyone, w, 1, 0).astype(jnp.bfloat16) for w in (w_in, w_in_mate)], axis=1
        )

    some_kept = jnp.sum(counts) > 0
    tokens_all, hidden_terms = lax.cond(some_kept, forward, forward_plain, tokens_line)
    hidden = added_up(swapped(cut(hidden_terms, row_count), "row"))
    active, slope = gelu_both(hidden)
    slope_terms = jnp.concatenate(
        [product(scaled_all, w, 1, 1).astype(jnp.bfloat16) for w in (w_out, w_out_mate)], axis=1
    )
    share = jnp.broadcast_to(active.astype(jnp.bfloat16)[None], (row_count, *active.shape))
    mixed = swapped(jnp.concatenate([share, cut(slope_terms, row_count)], axis=2), "row")
    activated = mixed[:, :, : active.shape[1]].reshape(rows_all, -1)
    grad_share = (added_up(mixed[:, :, active.shape[1] :]) * slope).astype(jnp.bfloat16)
    output_terms = (
        product(activated[:, :units], w_out, 1, 0) + product(activated[:, units:], w_out_mate, 1, 0)
    ).astype(jnp.bfloat16)
    grad_share, output_terms = lax.optimization_barrier((grad_share, output_terms))
    output_line = lax.psum_scatter(output_terms, "col", scatter_dimension=0, tiled=True)

    def backward(share):
        hidden_grad = spread(share, "row", row_count).reshape(rows_all, -1)
        back_terms = (
            product(hidden_grad[:, :units], w_in, 1, 1)
            + product(hidden_grad[:, units:], w_in_mate, 1, 1)
        ).astype(jnp.bfloat16)
        back_line = added_up(swapped(cut(back_terms, columns), "col")).astype(jnp.bfloat16)
        w_out_grad = product(activated[:, :units], scaled_all, 0, 0) + product(
            mate(activated[:, units:]), mate(scaled_all), 0, 0
        )
        w_in_grad = product(tokens_all, hidden_grad[:, :units], 0, 0) + product(
            mate(tokens_all), mate(hidden_grad[:, units:]), 0, 0
        )
        return back_line, w_in_grad, w_out_grad

    def nothing(share):
        return (
            jnp.zeros((line_rows, width), jnp.bfloat16),
            jnp.zeros((width, units), jnp.float32),
            jnp.zeros((units, width), jnp.float32),
        )

    back_line, w_in_grad, w_out_grad = lax.cond(some_kept, backward, nothing, grad_share)
    ends = jnp.concatenate([cut(output_line, chips), cut(back_line, chips)], axis=1)
    finished = added_up(swapped(ends, "rep", same_core))
    block_output = (tokens_local.astype(jnp.float32) + finished[:rows_local]).astype(jnp.bfloat16)
    input_grad = (scaled.astype(jnp.float32) + finished[rows_local:]).astype(jnp.bfloat16)

    return (
        block_output.reshape(1, rows_local, width),
        input_grad.reshape(1, rows_local, width),
        w_in_grad,
        w_out_grad,
    )


def solution(mesh):
    placed = (
        P("rep", "col", "row"),
        P("row", ("rep", "col")),
        P(("rep", "col"), "row"),
        P("rep", "col", "row"),
        P(),
    )
    return jax.shard_map(
        body,
        mesh=mesh,
        in_specs=placed,
        out_specs=(
            P("rep", "col", "row"),
            P("rep", "col", "row"),
            P("row", ("rep", "col")),
            P(("rep", "col"), "row"),
        ),
        check_vma=False,
    )
```

```python
import jax
import jax.numpy as jnp
from jax import lax
from jax.sharding import PartitionSpec as P

MBT = 32
CORES = 2

root_coef = 0.7978845608028654
cubic_coef = 0.044715


def gelu_both(values):
    inner = root_coef * (values + cubic_coef * values * values * values)
    tangent = jnp.tanh(inner)
    slope = 0.5 * (1.0 + tangent) + 0.5 * values * (1.0 - tangent * tangent) * root_coef * (
        1.0 + 3.0 * cubic_coef * values * values
    )
    return 0.5 * values * (1.0 + tangent), slope


def product(left, right, left_dim, right_dim):
    return lax.dot_general(
        left, right, (((left_dim,), (right_dim,)), ((), ())), preferred_element_type=jnp.float32
    )


def cut(value, pieces):
    rows, width = value.shape
    return value.reshape(pieces, rows // pieces, width)


def swapped(value, axis):
    return lax.all_to_all(value, axis, 0, 0, tiled=True)


def added_up(pieces):
    total = pieces[0].astype(jnp.float32)
    for at in range(1, len(pieces)):
        total = total + pieces[at].astype(jnp.float32)
    return total


def spread(value, axis, size):
    return swapped(jnp.broadcast_to(value[None], (size, *value.shape)), axis)


def body(inputs, w_in, w_out, cotangent, counts):
    rows_local = inputs.shape[1]
    width = inputs.shape[2]
    units = w_in.shape[1]
    replicas = lax.axis_size("rep")
    columns = lax.axis_size("col")
    row_count = lax.axis_size("row")
    chips = replicas // CORES
    to_mate = [(r, r // CORES * CORES + (r + 1) % CORES) for r in range(replicas)]
    mate = lambda value: lax.ppermute(value, "rep", to_mate)

    tokens_local = inputs.reshape(rows_local, width)
    replica_index = lax.axis_index("rep")
    column_index = lax.axis_index("col")
    own_count = jnp.sum(jnp.where(jnp.arange(replicas) == replica_index, counts, 0))
    token_total = (MBT * jnp.sum(counts)).astype(jnp.float32)
    positions = column_index * rows_local + jnp.arange(rows_local, dtype=jnp.int32)
    kept_mask = (positions // MBT < own_count).astype(jnp.float32)
    scaled = (
        cotangent.reshape(rows_local, width).astype(jnp.float32)
        * kept_mask[:, None]
        / token_total
    ).astype(jnp.bfloat16)

    w_in_mate, w_out_mate = mate(w_in), mate(w_out)

    onward = lambda value, k: lax.ppermute(
        value, "rep", [(r, (r + k * CORES) % replicas) for r in range(replicas)]
    )
    scaled_ring = spread(scaled, "col", columns)
    tokens_line = jnp.stack([tokens_local] + [onward(tokens_local, k) for k in range(1, chips)])
    rows_all = columns * chips * rows_local
    tokens_all = spread(tokens_line.reshape(-1, width), "col", columns).reshape(rows_all, width)
    scaled_all = jnp.stack(
        [scaled_ring] + [onward(scaled_ring, k) for k in range(1, chips)], axis=1
    ).reshape(rows_all, width)

    def pair(left, rights, right_dim):
        return [product(left, w, 1, right_dim).astype(jnp.bfloat16) for w in rights]

    terms = jnp.concatenate(
        pair(tokens_all, (w_in, w_in_mate), 0) + pair(scaled_all, (w_out, w_out_mate), 1), axis=1
    )
    sums = added_up(swapped(cut(terms, row_count), "row"))
    active, slope = gelu_both(sums[:, : 2 * units])
    shares = jnp.concatenate(
        [active.astype(jnp.bfloat16), (sums[:, 2 * units :] * slope).astype(jnp.bfloat16)], axis=1
    )
    shares_all = spread(shares, "row", row_count).reshape(rows_all, 4 * units)
    active_own, active_other, grad_own, grad_other = [
        shares_all[:, at * units : (at + 1) * units] for at in range(4)
    ]

    back_terms = (
        product(grad_own, w_in, 1, 1) + product(grad_other, w_in_mate, 1, 1)
    ).astype(jnp.bfloat16)
    output_terms = (
        product(active_own, w_out, 1, 0) + product(active_other, w_out_mate, 1, 0)
    ).astype(jnp.bfloat16)

    output_line = added_up(swapped(cut(output_terms, columns), "col")).astype(jnp.bfloat16)
    back_blocks = back_terms.reshape(columns, chips, rows_local, width)
    back_ring = added_up(
        [back_blocks[:, 0]] + [onward(back_blocks[:, k], chips - k) for k in range(1, chips)]
    ).astype(jnp.bfloat16)
    output_blocks = output_line.reshape(chips, rows_local, width)
    mixed = added_up(
        [output_blocks[0]] + [onward(output_blocks[k], chips - k) for k in range(1, chips)]
    )
    back = added_up(swapped(back_ring, "col"))
    block_output = (tokens_local.astype(jnp.float32) + mixed).astype(jnp.bfloat16)
    input_grad = (scaled.astype(jnp.float32) + back).astype(jnp.bfloat16)

    w_in_grad = product(tokens_all, grad_own, 0, 0) + product(
        mate(tokens_all), mate(grad_other), 0, 0
    )
    w_out_grad = product(active_own, scaled_all, 0, 0) + product(
        mate(active_other), mate(scaled_all), 0, 0
    )
    return (
        block_output.reshape(1, rows_local, width),
        input_grad.reshape(1, rows_local, width),
        w_in_grad,
        w_out_grad,
    )


def solution(mesh):
    placed = (
        P("rep", "col", "row"),
        P("row", ("rep", "col")),
        P(("rep", "col"), "row"),
        P("rep", "col", "row"),
        P(),
    )
    return jax.shard_map(
        body,
        mesh=mesh,
        in_specs=placed,
        out_specs=(
            P("rep", "col", "row"),
            P("rep", "col", "row"),
            P("row", ("rep", "col")),
            P(("rep", "col"), "row"),
        ),
        check_vma=False,
    )
```

```python
import jax
import jax.numpy as jnp
from jax import lax
from jax.sharding import PartitionSpec as P

MBT = 32
CORES = 2

root_coef = 0.7978845608028654
cubic_coef = 0.044715


def gelu_both(values):
    inner = root_coef * (values + cubic_coef * values * values * values)
    tangent = jnp.tanh(inner)
    slope = 0.5 * (1.0 + tangent) + 0.5 * values * (1.0 - tangent * tangent) * root_coef * (
        1.0 + 3.0 * cubic_coef * values * values
    )
    return 0.5 * values * (1.0 + tangent), slope


def product(left, right, left_dim, right_dim):
    return lax.dot_general(
        left, right, (((left_dim,), (right_dim,)), ((), ())), preferred_element_type=jnp.float32
    )


def cut(value, pieces):
    rows, width = value.shape
    return value.reshape(pieces, rows // pieces, width)


def swapped(value, axis, groups=None):
    return lax.all_to_all(value, axis, 0, 0, axis_index_groups=groups, tiled=True)


def added_up(pieces):
    total = pieces[0].astype(jnp.float32)
    for at in range(1, pieces.shape[0]):
        total = total + pieces[at].astype(jnp.float32)
    return total


def spread(value, axis, size, groups=None):
    return swapped(jnp.broadcast_to(value[None], (size, *value.shape)), axis, groups)


def body(inputs, w_in, w_out, cotangent, counts):
    rows_local = inputs.shape[1]
    width = inputs.shape[2]
    units = w_in.shape[1]
    replicas = lax.axis_size("rep")
    columns = lax.axis_size("col")
    row_count = lax.axis_size("row")
    chips = replicas // CORES
    same_core = [[chip * CORES + core for chip in range(chips)] for core in range(CORES)]
    to_mate = [(r, r // CORES * CORES + (r + 1) % CORES) for r in range(replicas)]
    mate = lambda value: lax.ppermute(value, "rep", to_mate)

    tokens_local = inputs.reshape(rows_local, width)
    replica_index = lax.axis_index("rep")
    column_index = lax.axis_index("col")
    own_count = jnp.sum(jnp.where(jnp.arange(replicas) == replica_index, counts, 0))
    token_total = (MBT * jnp.sum(counts)).astype(jnp.float32)
    positions = column_index * rows_local + jnp.arange(rows_local, dtype=jnp.int32)
    kept_mask = (positions // MBT < own_count).astype(jnp.float32)
    w_in_mate, w_out_mate = mate(w_in), mate(w_out)

    line_rows = chips * rows_local
    rows_all = columns * line_rows

    plane = [
        [(chip * CORES + core) * columns + column for column in range(columns) for chip in range(chips)]
        for core in range(CORES)
    ]
    tokens_all = spread(tokens_local, ("rep", "col"), columns * chips, plane).reshape(rows_all, width)

    onward = lambda value, k: lax.ppermute(
        value, "rep", [(r, (r + k * CORES) % replicas) for r in range(replicas)]
    )
    some_kept = jnp.sum(counts) > 0

    def gradient_line(cotangent_block):
        scaled = (
            cotangent_block.reshape(rows_local, width).astype(jnp.float32)
            * kept_mask[:, None]
            / token_total
        ).astype(jnp.bfloat16)
        near = [scaled] + [onward(scaled, k) for k in range(1, chips)]
        back = lax.rem(lax.div(replica_index, CORES) + chips, chips)
        ordered = []
        for place in range(chips):
            steps = lax.rem(back - place + chips, chips)
            block = near[0]
            for k in range(1, chips):
                block = jnp.where(steps == k, near[k], block)
            ordered.append(block)
        return scaled, jnp.concatenate(ordered + ordered[: chips // 2], axis=0)

    def no_gradient_line(cotangent_block):
        return (
            jnp.zeros((rows_local, width), jnp.bfloat16),
            jnp.zeros((line_rows * 3 // 2, width), jnp.bfloat16),
        )

    scaled, padded = lax.cond(some_kept, gradient_line, no_gradient_line, cotangent)
    scaled_all = lax.all_gather(padded, "col", axis=0)[:, :line_rows].reshape(rows_all, width)

    hidden_terms = jnp.concatenate(
        [product(tokens_all, w, 1, 0).astype(jnp.bfloat16) for w in (w_in, w_in_mate)], axis=1
    )
    hidden = added_up(swapped(cut(hidden_terms, row_count), "row"))
    active, slope = gelu_both(hidden)
    slope_terms = jnp.concatenate(
        [product(scaled_all, w, 1, 1).astype(jnp.bfloat16) for w in (w_out, w_out_mate)], axis=1
    )
    share = jnp.broadcast_to(active.astype(jnp.bfloat16)[None], (row_count, *active.shape))
    mixed = swapped(jnp.concatenate([share, cut(slope_terms, row_count)], axis=2), "row")
    activated = mixed[:, :, : active.shape[1]].reshape(rows_all, -1)
    grad_share = (added_up(mixed[:, :, active.shape[1] :]) * slope).astype(jnp.bfloat16)
    output_terms = (
        product(activated[:, :units], w_out, 1, 0) + product(activated[:, units:], w_out_mate, 1, 0)
    ).astype(jnp.bfloat16)
    grad_share, output_terms = lax.optimization_barrier((grad_share, output_terms))
    output_line = lax.psum_scatter(output_terms, "col", scatter_dimension=0, tiled=True)

    def backward(share):
        hidden_grad = spread(share, "row", row_count).reshape(rows_all, -1)
        back_terms = (
            product(hidden_grad[:, :units], w_in, 1, 1)
            + product(hidden_grad[:, units:], w_in_mate, 1, 1)
        ).astype(jnp.bfloat16)
        back_line = added_up(swapped(cut(back_terms, columns), "col")).astype(jnp.bfloat16)
        w_out_grad = product(activated[:, :units], scaled_all, 0, 0) + product(
            mate(activated[:, units:]), mate(scaled_all), 0, 0
        )
        w_in_grad = product(tokens_all, hidden_grad[:, :units], 0, 0) + product(
            mate(tokens_all), mate(hidden_grad[:, units:]), 0, 0
        )
        return back_line, w_in_grad, w_out_grad

    def nothing(share):
        return (
            jnp.zeros((line_rows, width), jnp.bfloat16),
            jnp.zeros((width, units), jnp.float32),
            jnp.zeros((units, width), jnp.float32),
        )

    back_line, w_in_grad, w_out_grad = lax.cond(some_kept, backward, nothing, grad_share)
    ends = jnp.concatenate([cut(output_line, chips), cut(back_line, chips)], axis=1)
    finished = added_up(swapped(ends, "rep", same_core))
    block_output = (tokens_local.astype(jnp.float32) + finished[:rows_local]).astype(jnp.bfloat16)
    input_grad = (scaled.astype(jnp.float32) + finished[rows_local:]).astype(jnp.bfloat16)

    return (
        block_output.reshape(1, rows_local, width),
        input_grad.reshape(1, rows_local, width),
        w_in_grad,
        w_out_grad,
    )


def solution(mesh):
    placed = (
        P("rep", "col", "row"),
        P("row", ("rep", "col")),
        P(("rep", "col"), "row"),
        P("rep", "col", "row"),
        P(),
    )
    return jax.shard_map(
        body,
        mesh=mesh,
        in_specs=placed,
        out_specs=(
            P("rep", "col", "row"),
            P("rep", "col", "row"),
            P("row", ("rep", "col")),
            P(("rep", "col"), "row"),
        ),
        check_vma=False,
    )
```

```python
import jax
import jax.numpy as jnp
from jax import lax
from jax.experimental import pallas as pl
from jax.experimental.pallas import tpu as pltpu
from jax.sharding import PartitionSpec as P

MBT = 32
CORES = 2
VMEM = 24 << 20

root_coef = 0.7978845608028654
cubic_coef = 0.044715


def gelu_both(values):
    inner = root_coef * (values + cubic_coef * values * values * values)
    tangent = jnp.tanh(inner)
    slope = 0.5 * (1.0 + tangent) + 0.5 * values * (1.0 - tangent * tangent) * root_coef * (
        1.0 + 3.0 * cubic_coef * values * values
    )
    return 0.5 * values * (1.0 + tangent), slope


def product(left, right, left_dim, right_dim):
    return lax.dot_general(
        left, right, (((left_dim,), (right_dim,)), ((), ())), preferred_element_type=jnp.float32
    )


def paired(blocks, half, own, other, turned):
    count, rows, width = blocks.shape
    rows //= 2
    columns = own.shape[0] if turned else own.shape[1]
    step = count // 4

    def kernel(left_ref, own_ref, other_ref, out_ref):
        for at in range(4):
            left = left_ref[at * step : (at + 1) * step].reshape(step * rows, width)
            for place, right_ref in enumerate((own_ref, other_ref)):
                out_ref[
                    at * step * rows : (at + 1) * step * rows,
                    place * columns : (place + 1) * columns,
                ] = product(left, right_ref[...], 1, 1 if turned else 0).astype(jnp.bfloat16)

    return pl.pallas_call(
        kernel,
        grid=(1,),
        in_specs=[
            pl.BlockSpec((count, rows, width), lambda i: (0, half, 0)),
            pl.BlockSpec(own.shape, lambda i: (0, 0)),
            pl.BlockSpec(other.shape, lambda i: (0, 0)),
        ],
        out_specs=pl.BlockSpec((count * rows, 2 * columns), lambda i: (0, 0)),
        out_shape=jax.ShapeDtypeStruct((count * rows, 2 * columns), jnp.bfloat16),
        compiler_params=pltpu.CompilerParams(vmem_limit_bytes=VMEM),
        cost_estimate=pl.CostEstimate(
            flops=4 * count * rows * width * columns, bytes_accessed=4 << 20, transcendentals=0
        ),
    )(blocks, own, other)


def joined(blocks, own, other, turned):
    count, rows, _ = blocks.shape
    units, width = own.shape[::-1] if turned else own.shape
    step = count // 4

    def kernel(left_ref, own_ref, other_ref, out_ref):
        for at in range(4):
            left = left_ref[at * step : (at + 1) * step].reshape(step * rows, 2 * units)
            dim = 1 if turned else 0
            total = product(left[:, :units], own_ref[...], 1, dim)
            total = total + product(left[:, units:], other_ref[...], 1, dim)
            out_ref[at * step * rows : (at + 1) * step * rows] = total.astype(jnp.bfloat16)

    return pl.pallas_call(
        kernel,
        grid=(1,),
        in_specs=[
            pl.BlockSpec((count, rows, 2 * units), lambda i: (0, 0, 0)),
            pl.BlockSpec(own.shape, lambda i: (0, 0)),
            pl.BlockSpec(other.shape, lambda i: (0, 0)),
        ],
        out_specs=pl.BlockSpec((count * rows, width), lambda i: (0, 0)),
        out_shape=jax.ShapeDtypeStruct((count * rows, width), jnp.bfloat16),
        compiler_params=pltpu.CompilerParams(vmem_limit_bytes=VMEM),
        cost_estimate=pl.CostEstimate(
            flops=4 * count * rows * width * units, bytes_accessed=4 << 20, transcendentals=0
        ),
    )(blocks, own, other)


def cut(value, pieces):
    rows, width = value.shape
    return value.reshape(pieces, rows // pieces, width)


def swapped(value, axis, groups=None):
    return lax.all_to_all(value, axis, 0, 0, axis_index_groups=groups, tiled=True)


def added_up(pieces):
    total = pieces[0].astype(jnp.float32)
    for at in range(1, pieces.shape[0]):
        total = total + pieces[at].astype(jnp.float32)
    return total


def spread(value, axis, size, groups=None):
    return swapped(jnp.broadcast_to(value[None], (size, *value.shape)), axis, groups)


def body(inputs, w_in, w_out, cotangent, counts):
    rows_local = inputs.shape[1]
    width = inputs.shape[2]
    units = w_in.shape[1]
    replicas = lax.axis_size("rep")
    columns = lax.axis_size("col")
    row_count = lax.axis_size("row")
    chips = replicas // CORES
    same_core = [[chip * CORES + core for chip in range(chips)] for core in range(CORES)]
    to_mate = [(r, r // CORES * CORES + (r + 1) % CORES) for r in range(replicas)]
    mate = lambda value: lax.ppermute(value, "rep", to_mate)

    tokens_local = inputs.reshape(rows_local, width)
    replica_index = lax.axis_index("rep")
    column_index = lax.axis_index("col")
    own_count = jnp.sum(jnp.where(jnp.arange(replicas) == replica_index, counts, 0))
    token_total = (MBT * jnp.sum(counts)).astype(jnp.float32)
    positions = column_index * rows_local + jnp.arange(rows_local, dtype=jnp.int32)
    kept_mask = (positions // MBT < own_count).astype(jnp.float32)
    scaled = (
        cotangent.reshape(rows_local, width).astype(jnp.float32)
        * kept_mask[:, None]
        / token_total
    ).astype(jnp.bfloat16)

    w_in_mate, w_out_mate = mate(w_in), mate(w_out)

    line_rows = chips * rows_local
    rows_all = columns * line_rows

    plane = [
        [(chip * CORES + core) * columns + column for column in range(columns) for chip in range(chips)]
        for core in range(CORES)
    ]
    both = jnp.concatenate([tokens_local, scaled], axis=0)
    everyone = spread(both, ("rep", "col"), columns * chips, plane)
    hidden_terms = paired(everyone, 0, w_in, w_in_mate, False)
    slope_terms = paired(everyone, 1, w_out, w_out_mate, True)

    hidden = added_up(swapped(cut(hidden_terms, row_count), "row"))
    active, slope = gelu_both(hidden)
    share = jnp.broadcast_to(active.astype(jnp.bfloat16)[None], (row_count, *active.shape))
    mixed = swapped(jnp.concatenate([share, cut(slope_terms, row_count)], axis=2), "row")
    activated = mixed[:, :, : active.shape[1]].reshape(rows_all, -1)
    grad_share = (added_up(mixed[:, :, active.shape[1] :]) * slope).astype(jnp.bfloat16)
    output_terms = joined(mixed, w_out, w_out_mate, False)
    output_line = lax.psum_scatter(output_terms, "col", scatter_dimension=0, tiled=True)
    tokens_all, scaled_all = [
        everyone[:, at * rows_local : (at + 1) * rows_local].reshape(rows_all, width) for at in (0, 1)
    ]

    def backward(share):
        shares = spread(share, "row", row_count)
        back_terms = joined(shares, w_in, w_in_mate, True)
        hidden_grad = shares.reshape(rows_all, -1)
        back_line = added_up(swapped(cut(back_terms, columns), "col")).astype(jnp.bfloat16)
        w_out_grad = product(activated[:, :units], scaled_all, 0, 0) + product(
            mate(activated[:, units:]), mate(scaled_all), 0, 0
        )
        w_in_grad = product(tokens_all, hidden_grad[:, :units], 0, 0) + product(
            mate(tokens_all), mate(hidden_grad[:, units:]), 0, 0
        )
        return back_line, w_in_grad, w_out_grad

    def nothing(share):
        return (
            jnp.zeros((line_rows, width), jnp.bfloat16),
            jnp.zeros((width, units), jnp.float32),
            jnp.zeros((units, width), jnp.float32),
        )

    back_line, w_in_grad, w_out_grad = lax.cond(jnp.sum(counts) > 0, backward, nothing, grad_share)
    ends = jnp.concatenate([cut(output_line, chips), cut(back_line, chips)], axis=1)
    finished = added_up(swapped(ends, "rep", same_core))
    block_output = (tokens_local.astype(jnp.float32) + finished[:rows_local]).astype(jnp.bfloat16)
    input_grad = (scaled.astype(jnp.float32) + finished[rows_local:]).astype(jnp.bfloat16)

    return (
        block_output.reshape(1, rows_local, width),
        input_grad.reshape(1, rows_local, width),
        w_in_grad,
        w_out_grad,
    )


def solution(mesh):
    placed = (
        P("rep", "col", "row"),
        P("row", ("rep", "col")),
        P(("rep", "col"), "row"),
        P("rep", "col", "row"),
        P(),
    )
    return jax.shard_map(
        body,
        mesh=mesh,
        in_specs=placed,
        out_specs=(
            P("rep", "col", "row"),
            P("rep", "col", "row"),
            P("row", ("rep", "col")),
            P(("rep", "col"), "row"),
        ),
        check_vma=False,
    )
```

```python
import jax
import jax.numpy as jnp
from jax import lax
from jax.experimental import pallas as pl
from jax.experimental.pallas import tpu as pltpu
from jax.sharding import PartitionSpec as P

MBT = 32
CORES = 2
VMEM = 24 << 20

root_coef = 0.7978845608028654
cubic_coef = 0.044715


def gelu_both(values):
    inner = root_coef * (values + cubic_coef * values * values * values)
    tangent = jnp.tanh(inner)
    slope = 0.5 * (1.0 + tangent) + 0.5 * values * (1.0 - tangent * tangent) * root_coef * (
        1.0 + 3.0 * cubic_coef * values * values
    )
    return 0.5 * values * (1.0 + tangent), slope


def product(left, right, left_dim, right_dim):
    return lax.dot_general(
        left, right, (((left_dim,), (right_dim,)), ((), ())), preferred_element_type=jnp.float32
    )


def prepared(tokens, cotangent, counts, copies):
    _, rows, width = tokens.shape

    def kernel(counts_ref, tokens_ref, cotangent_ref, send_ref, scaled_ref):
        own_count = counts_ref[lax.axis_index("rep")]
        total = counts_ref[0]
        for replica in range(1, counts.shape[0]):
            total = total + counts_ref[replica]
        token_total = (MBT * total).astype(jnp.float32)
        positions = lax.axis_index("col") * rows + lax.broadcasted_iota(
            jnp.int32, (rows, width), 0
        )
        kept_mask = (positions < MBT * own_count).astype(jnp.float32)
        scaled = (cotangent_ref[0].astype(jnp.float32) * kept_mask / token_total).astype(
            jnp.bfloat16
        )
        scaled_ref[...] = scaled
        for copy in range(copies):
            send_ref[copy, :rows] = tokens_ref[0]
            send_ref[copy, rows:] = scaled

    return pl.pallas_call(
        kernel,
        in_specs=[
            pl.BlockSpec(memory_space=pltpu.SMEM),
            pl.BlockSpec(memory_space=pltpu.VMEM),
            pl.BlockSpec(memory_space=pltpu.VMEM),
        ],
        out_specs=[pl.BlockSpec(memory_space=pltpu.VMEM), pl.BlockSpec(memory_space=pltpu.VMEM)],
        out_shape=[
            jax.ShapeDtypeStruct((copies, 2 * rows, width), jnp.bfloat16),
            jax.ShapeDtypeStruct((rows, width), jnp.bfloat16),
        ],
    )(counts, tokens, cotangent)


def paired(blocks, rows, own, other, turned):
    count, _, width = blocks.shape
    columns = own.shape[0] if turned else own.shape[1]
    step = count // 4

    def kernel(left_ref, own_ref, other_ref, out_ref):
        for at in range(4):
            left = left_ref[at * step : (at + 1) * step].reshape(step * rows, width)
            for place, right_ref in enumerate((own_ref, other_ref)):
                out_ref[
                    at * step * rows : (at + 1) * step * rows,
                    place * columns : (place + 1) * columns,
                ] = product(left, right_ref[...], 1, 1 if turned else 0).astype(jnp.bfloat16)

    return pl.pallas_call(
        kernel,
        grid=(1,),
        in_specs=[
            pl.BlockSpec((count, rows, width), lambda i: (0, 0, 0)),
            pl.BlockSpec(own.shape, lambda i: (0, 0)),
            pl.BlockSpec(other.shape, lambda i: (0, 0)),
        ],
        out_specs=pl.BlockSpec((count * rows, 2 * columns), lambda i: (0, 0)),
        out_shape=jax.ShapeDtypeStruct((count * rows, 2 * columns), jnp.bfloat16),
        compiler_params=pltpu.CompilerParams(vmem_limit_bytes=VMEM),
        cost_estimate=pl.CostEstimate(
            flops=4 * count * rows * width * columns, bytes_accessed=4 << 20, transcendentals=0
        ),
    )(blocks, own, other)


def joined(blocks, own, other, turned):
    count, rows, _ = blocks.shape
    units, width = own.shape[::-1] if turned else own.shape
    step = count // 4

    def kernel(left_ref, own_ref, other_ref, out_ref):
        for at in range(4):
            left = left_ref[at * step : (at + 1) * step].reshape(step * rows, 2 * units)
            dim = 1 if turned else 0
            total = product(left[:, :units], own_ref[...], 1, dim)
            total = total + product(left[:, units:], other_ref[...], 1, dim)
            out_ref[at * step * rows : (at + 1) * step * rows] = total.astype(jnp.bfloat16)

    return pl.pallas_call(
        kernel,
        grid=(1,),
        in_specs=[
            pl.BlockSpec((count, rows, 2 * units), lambda i: (0, 0, 0)),
            pl.BlockSpec(own.shape, lambda i: (0, 0)),
            pl.BlockSpec(other.shape, lambda i: (0, 0)),
        ],
        out_specs=pl.BlockSpec((count * rows, width), lambda i: (0, 0)),
        out_shape=jax.ShapeDtypeStruct((count * rows, width), jnp.bfloat16),
        compiler_params=pltpu.CompilerParams(vmem_limit_bytes=VMEM),
        cost_estimate=pl.CostEstimate(
            flops=4 * count * rows * width * units, bytes_accessed=4 << 20, transcendentals=0
        ),
    )(blocks, own, other)


def cut(value, pieces):
    rows, width = value.shape
    return value.reshape(pieces, rows // pieces, width)


def swapped(value, axis, groups=None):
    return lax.all_to_all(value, axis, 0, 0, axis_index_groups=groups, tiled=True)


def added_up(pieces):
    total = pieces[0].astype(jnp.float32)
    for at in range(1, pieces.shape[0]):
        total = total + pieces[at].astype(jnp.float32)
    return total


def spread(value, axis, size, groups=None):
    return swapped(jnp.broadcast_to(value[None], (size, *value.shape)), axis, groups)


def body(inputs, w_in, w_out, cotangent, counts):
    rows_local = inputs.shape[1]
    width = inputs.shape[2]
    units = w_in.shape[1]
    replicas = lax.axis_size("rep")
    columns = lax.axis_size("col")
    row_count = lax.axis_size("row")
    chips = replicas // CORES
    same_core = [[chip * CORES + core for chip in range(chips)] for core in range(CORES)]
    to_mate = [(r, r // CORES * CORES + (r + 1) % CORES) for r in range(replicas)]
    mate = lambda value: lax.ppermute(value, "rep", to_mate)

    tokens_local = inputs.reshape(rows_local, width)
    send, scaled = prepared(inputs, cotangent, counts, chips)

    w_in_mate, w_out_mate = mate(w_in), mate(w_out)

    line = swapped(send, "rep", same_core)
    tokens_line = line[:, :rows_local].reshape(chips * rows_local, width)
    scaled_line = line[:, rows_local:].reshape(chips * rows_local, width)
    line_rows = chips * rows_local
    rows_all = columns * line_rows

    padded = jnp.concatenate([scaled_line, scaled_line[: line_rows // 2]], axis=0)
    scaled_blocks = lax.all_gather(padded, "col", axis=0)

    def forward(line):
        blocks = spread(line, "col", columns)
        return blocks, paired(blocks, line_rows, w_in, w_in_mate, False)

    def forward_plain(line):
        blocks = lax.all_gather(line, "col", axis=0)
        return blocks, paired(blocks, line_rows, w_in, w_in_mate, False)

    some_kept = jnp.sum(counts) > 0
    tokens_blocks, hidden_terms = lax.cond(some_kept, forward, forward_plain, tokens_line)
    slope_terms = paired(scaled_blocks, line_rows, w_out, w_out_mate, True)

    hidden = added_up(swapped(cut(hidden_terms, row_count), "row"))
    active, slope = gelu_both(hidden)
    share = jnp.broadcast_to(active.astype(jnp.bfloat16)[None], (row_count, *active.shape))
    mixed = swapped(jnp.concatenate([share, cut(slope_terms, row_count)], axis=2), "row")
    activated = mixed[:, :, : active.shape[1]].reshape(rows_all, -1)
    grad_share = (added_up(mixed[:, :, active.shape[1] :]) * slope).astype(jnp.bfloat16)
    output_terms = joined(mixed, w_out, w_out_mate, False)
    output_line = lax.psum_scatter(output_terms, "col", scatter_dimension=0, tiled=True)
    tokens_all = tokens_blocks.reshape(rows_all, width)
    scaled_all = scaled_blocks[:, :line_rows].reshape(rows_all, width)

    def backward(share):
        shares = spread(share, "row", row_count)
        back_terms = joined(shares, w_in, w_in_mate, True)
        hidden_grad = shares.reshape(rows_all, -1)
        back_line = added_up(swapped(cut(back_terms, columns), "col")).astype(jnp.bfloat16)
        w_out_grad = product(activated[:, :units], scaled_all, 0, 0) + product(
            mate(activated[:, units:]), mate(scaled_all), 0, 0
        )
        w_in_grad = product(tokens_all, hidden_grad[:, :units], 0, 0) + product(
            mate(tokens_all), mate(hidden_grad[:, units:]), 0, 0
        )
        return back_line, w_in_grad, w_out_grad

    def nothing(share):
        return (
            jnp.zeros((line_rows, width), jnp.bfloat16),
            jnp.zeros((width, units), jnp.float32),
            jnp.zeros((units, width), jnp.float32),
        )

    back_line, w_in_grad, w_out_grad = lax.cond(some_kept, backward, nothing, grad_share)
    ends = jnp.concatenate([cut(output_line, chips), cut(back_line, chips)], axis=1)
    finished = added_up(swapped(ends, "rep", same_core))
    block_output = (tokens_local.astype(jnp.float32) + finished[:rows_local]).astype(jnp.bfloat16)
    input_grad = (scaled.astype(jnp.float32) + finished[rows_local:]).astype(jnp.bfloat16)

    return (
        block_output.reshape(1, rows_local, width),
        input_grad.reshape(1, rows_local, width),
        w_in_grad,
        w_out_grad,
    )


def solution(mesh):
    placed = (
        P("rep", "col", "row"),
        P("row", ("rep", "col")),
        P(("rep", "col"), "row"),
        P("rep", "col", "row"),
        P(),
    )
    return jax.shard_map(
        body,
        mesh=mesh,
        in_specs=placed,
        out_specs=(
            P("rep", "col", "row"),
            P("rep", "col", "row"),
            P("row", ("rep", "col")),
            P(("rep", "col"), "row"),
        ),
        check_vma=False,
    )
```

```python
import jax
import jax.numpy as jnp
from jax import lax
from jax.experimental import pallas as pl
from jax.experimental.pallas import tpu as pltpu
from jax.sharding import PartitionSpec as P

MBT = 32
CORES = 2
VMEM = 24 << 20

root_coef = 0.7978845608028654
cubic_coef = 0.044715


def gelu_both(values):
    inner = root_coef * (values + cubic_coef * values * values * values)
    tangent = jnp.tanh(inner)
    slope = 0.5 * (1.0 + tangent) + 0.5 * values * (1.0 - tangent * tangent) * root_coef * (
        1.0 + 3.0 * cubic_coef * values * values
    )
    return 0.5 * values * (1.0 + tangent), slope


def product(left, right, left_dim, right_dim):
    return lax.dot_general(
        left, right, (((left_dim,), (right_dim,)), ((), ())), preferred_element_type=jnp.float32
    )


def prepared(tokens, cotangent, counts, copies):
    _, rows, width = tokens.shape

    def kernel(counts_ref, tokens_ref, cotangent_ref, send_ref, scaled_ref):
        own_count = counts_ref[lax.axis_index("rep")]
        total = counts_ref[0]
        for replica in range(1, counts.shape[0]):
            total = total + counts_ref[replica]
        token_total = (MBT * total).astype(jnp.float32)
        positions = lax.axis_index("col") * rows + lax.broadcasted_iota(
            jnp.int32, (rows, width), 0
        )
        kept_mask = (positions < MBT * own_count).astype(jnp.float32)
        scaled = (cotangent_ref[0].astype(jnp.float32) * kept_mask / token_total).astype(
            jnp.bfloat16
        )
        scaled_ref[...] = scaled
        for copy in range(copies):
            send_ref[copy, :rows] = tokens_ref[0]
            send_ref[copy, rows:] = scaled

    return pl.pallas_call(
        kernel,
        in_specs=[
            pl.BlockSpec(memory_space=pltpu.SMEM),
            pl.BlockSpec(memory_space=pltpu.VMEM),
            pl.BlockSpec(memory_space=pltpu.VMEM),
        ],
        out_specs=[pl.BlockSpec(memory_space=pltpu.VMEM), pl.BlockSpec(memory_space=pltpu.VMEM)],
        out_shape=[
            jax.ShapeDtypeStruct((copies, 2 * rows, width), jnp.bfloat16),
            jax.ShapeDtypeStruct((rows, width), jnp.bfloat16),
        ],
    )(counts, tokens, cotangent)


def paired(blocks, rows, own, other, turned):
    count, _, width = blocks.shape
    columns = own.shape[0] if turned else own.shape[1]
    step = count // 4

    def kernel(left_ref, own_ref, other_ref, out_ref):
        for at in range(4):
            left = left_ref[at * step : (at + 1) * step].reshape(step * rows, width)
            for place, right_ref in enumerate((own_ref, other_ref)):
                out_ref[
                    at * step * rows : (at + 1) * step * rows,
                    place * columns : (place + 1) * columns,
                ] = product(left, right_ref[...], 1, 1 if turned else 0).astype(jnp.bfloat16)

    return pl.pallas_call(
        kernel,
        grid=(1,),
        in_specs=[
            pl.BlockSpec((count, rows, width), lambda i: (0, 0, 0)),
            pl.BlockSpec(own.shape, lambda i: (0, 0)),
            pl.BlockSpec(other.shape, lambda i: (0, 0)),
        ],
        out_specs=pl.BlockSpec((count * rows, 2 * columns), lambda i: (0, 0)),
        out_shape=jax.ShapeDtypeStruct((count * rows, 2 * columns), jnp.bfloat16),
        compiler_params=pltpu.CompilerParams(vmem_limit_bytes=VMEM),
        cost_estimate=pl.CostEstimate(
            flops=4 * count * rows * width * columns, bytes_accessed=4 << 20, transcendentals=0
        ),
    )(blocks, own, other)


def joined(blocks, own, other, turned):
    count, rows, _ = blocks.shape
    units, width = own.shape[::-1] if turned else own.shape
    step = count // 4

    def kernel(left_ref, own_ref, other_ref, out_ref):
        for at in range(4):
            left = left_ref[at * step : (at + 1) * step].reshape(step * rows, 2 * units)
            dim = 1 if turned else 0
            total = product(left[:, :units], own_ref[...], 1, dim)
            total = total + product(left[:, units:], other_ref[...], 1, dim)
            out_ref[at * step * rows : (at + 1) * step * rows] = total.astype(jnp.bfloat16)

    return pl.pallas_call(
        kernel,
        grid=(1,),
        in_specs=[
            pl.BlockSpec((count, rows, 2 * units), lambda i: (0, 0, 0)),
            pl.BlockSpec(own.shape, lambda i: (0, 0)),
            pl.BlockSpec(other.shape, lambda i: (0, 0)),
        ],
        out_specs=pl.BlockSpec((count * rows, width), lambda i: (0, 0)),
        out_shape=jax.ShapeDtypeStruct((count * rows, width), jnp.bfloat16),
        compiler_params=pltpu.CompilerParams(vmem_limit_bytes=VMEM),
        cost_estimate=pl.CostEstimate(
            flops=4 * count * rows * width * units, bytes_accessed=4 << 20, transcendentals=0
        ),
    )(blocks, own, other)


def cut(value, pieces):
    rows, width = value.shape
    return value.reshape(pieces, rows // pieces, width)


def swapped(value, axis, groups=None):
    return lax.all_to_all(value, axis, 0, 0, axis_index_groups=groups, tiled=True)


def added_up(pieces):
    total = pieces[0].astype(jnp.float32)
    for at in range(1, pieces.shape[0]):
        total = total + pieces[at].astype(jnp.float32)
    return total


def spread(value, axis, size, groups=None):
    return swapped(jnp.broadcast_to(value[None], (size, *value.shape)), axis, groups)


def body(inputs, w_in, w_out, cotangent, counts):
    rows_local = inputs.shape[1]
    width = inputs.shape[2]
    units = w_in.shape[1]
    replicas = lax.axis_size("rep")
    columns = lax.axis_size("col")
    row_count = lax.axis_size("row")
    chips = replicas // CORES
    same_core = [[chip * CORES + core for chip in range(chips)] for core in range(CORES)]
    to_mate = [(r, r // CORES * CORES + (r + 1) % CORES) for r in range(replicas)]
    mate = lambda value: lax.ppermute(value, "rep", to_mate)

    tokens_local = inputs.reshape(rows_local, width)
    send, scaled = prepared(inputs, cotangent, counts, chips)

    w_in_mate, w_out_mate = mate(w_in), mate(w_out)

    line = swapped(send, "rep", same_core)
    tokens_line = line[:, :rows_local].reshape(chips * rows_local, width)
    scaled_line = line[:, rows_local:].reshape(chips * rows_local, width)
    line_rows = chips * rows_local
    rows_all = columns * line_rows

    padded = jnp.concatenate([scaled_line, scaled_line[: line_rows * 3 // 8]], axis=0)
    scaled_blocks = lax.all_gather(padded, "col", axis=0)

    def forward(line):
        blocks = spread(line, "col", columns)
        return blocks, paired(blocks, line_rows, w_in, w_in_mate, False)

    def forward_plain(line):
        blocks = lax.all_gather(line, "col", axis=0)
        return blocks, paired(blocks, line_rows, w_in, w_in_mate, False)

    some_kept = jnp.sum(counts) > 0
    tokens_blocks, hidden_terms = lax.cond(some_kept, forward_plain, forward, tokens_line)
    slope_terms = paired(scaled_blocks, line_rows, w_out, w_out_mate, True)

    hidden = added_up(swapped(cut(hidden_terms, row_count), "row"))
    active, slope = gelu_both(hidden)
    share = jnp.broadcast_to(active.astype(jnp.bfloat16)[None], (row_count, *active.shape))
    mixed = swapped(jnp.concatenate([share, cut(slope_terms, row_count)], axis=2), "row")
    activated = mixed[:, :, : active.shape[1]].reshape(rows_all, -1)
    grad_share = (added_up(mixed[:, :, active.shape[1] :]) * slope).astype(jnp.bfloat16)
    output_terms = joined(mixed, w_out, w_out_mate, False)
    output_line = lax.psum_scatter(output_terms, "col", scatter_dimension=0, tiled=True)
    tokens_all = tokens_blocks.reshape(rows_all, width)
    scaled_all = scaled_blocks[:, :line_rows].reshape(rows_all, width)

    def backward(share):
        shares = spread(share, "row", row_count)
        back_terms = joined(shares, w_in, w_in_mate, True)
        hidden_grad = shares.reshape(rows_all, -1)
        back_line = added_up(swapped(cut(back_terms, columns), "col")).astype(jnp.bfloat16)
        w_out_grad = product(activated[:, :units], scaled_all, 0, 0) + product(
            mate(activated[:, units:]), mate(scaled_all), 0, 0
        )
        w_in_grad = product(tokens_all, hidden_grad[:, :units], 0, 0) + product(
            mate(tokens_all), mate(hidden_grad[:, units:]), 0, 0
        )
        return back_line, w_in_grad, w_out_grad

    def nothing(share):
        return (
            jnp.zeros((line_rows, width), jnp.bfloat16),
            jnp.zeros((width, units), jnp.float32),
            jnp.zeros((units, width), jnp.float32),
        )

    back_line, w_in_grad, w_out_grad = lax.cond(some_kept, backward, nothing, grad_share)
    ends = jnp.concatenate([cut(output_line, chips), cut(back_line, chips)], axis=1)
    finished = added_up(swapped(ends, "rep", same_core))
    block_output = (tokens_local.astype(jnp.float32) + finished[:rows_local]).astype(jnp.bfloat16)
    input_grad = (scaled.astype(jnp.float32) + finished[rows_local:]).astype(jnp.bfloat16)

    return (
        block_output.reshape(1, rows_local, width),
        input_grad.reshape(1, rows_local, width),
        w_in_grad,
        w_out_grad,
    )


def solution(mesh):
    placed = (
        P("rep", "col", "row"),
        P("row", ("rep", "col")),
        P(("rep", "col"), "row"),
        P("rep", "col", "row"),
        P(),
    )
    return jax.shard_map(
        body,
        mesh=mesh,
        in_specs=placed,
        out_specs=(
            P("rep", "col", "row"),
            P("rep", "col", "row"),
            P("row", ("rep", "col")),
            P(("rep", "col"), "row"),
        ),
        check_vma=False,
    )
```

```python
import jax
import jax.numpy as jnp
from jax import lax
from jax.experimental import pallas as pl
from jax.experimental.pallas import tpu as pltpu
from jax.sharding import PartitionSpec as P

MBT = 32
CORES = 2
VMEM = 24 << 20

root_coef = 0.7978845608028654
cubic_coef = 0.044715


def gelu_both(values):
    inner = root_coef * (values + cubic_coef * values * values * values)
    tangent = jnp.tanh(inner)
    slope = 0.5 * (1.0 + tangent) + 0.5 * values * (1.0 - tangent * tangent) * root_coef * (
        1.0 + 3.0 * cubic_coef * values * values
    )
    return 0.5 * values * (1.0 + tangent), slope


def product(left, right, left_dim, right_dim):
    return lax.dot_general(
        left, right, (((left_dim,), (right_dim,)), ((), ())), preferred_element_type=jnp.float32
    )


def prepared(tokens, cotangent, counts, copies):
    _, rows, width = tokens.shape

    def kernel(counts_ref, tokens_ref, cotangent_ref, send_ref, scaled_ref):
        own_count = counts_ref[lax.axis_index("rep")]
        total = counts_ref[0]
        for replica in range(1, counts.shape[0]):
            total = total + counts_ref[replica]
        token_total = (MBT * total).astype(jnp.float32)
        positions = lax.axis_index("col") * rows + lax.broadcasted_iota(
            jnp.int32, (rows, width), 0
        )
        kept_mask = (positions < MBT * own_count).astype(jnp.float32)
        scaled = (cotangent_ref[0].astype(jnp.float32) * kept_mask / token_total).astype(
            jnp.bfloat16
        )
        scaled_ref[...] = scaled
        for copy in range(copies):
            send_ref[copy, :rows] = tokens_ref[0]
            send_ref[copy, rows:] = scaled

    return pl.pallas_call(
        kernel,
        in_specs=[
            pl.BlockSpec(memory_space=pltpu.SMEM),
            pl.BlockSpec(memory_space=pltpu.VMEM),
            pl.BlockSpec(memory_space=pltpu.VMEM),
        ],
        out_specs=[pl.BlockSpec(memory_space=pltpu.VMEM), pl.BlockSpec(memory_space=pltpu.VMEM)],
        out_shape=[
            jax.ShapeDtypeStruct((copies, 2 * rows, width), jnp.bfloat16),
            jax.ShapeDtypeStruct((rows, width), jnp.bfloat16),
        ],
    )(counts, tokens, cotangent)


def paired(blocks, rows, own, other, turned):
    count, _, width = blocks.shape
    columns = own.shape[0] if turned else own.shape[1]
    step = count // 4

    def kernel(left_ref, own_ref, other_ref, out_ref):
        for at in range(4):
            left = left_ref[at * step : (at + 1) * step].reshape(step * rows, width)
            for place, right_ref in enumerate((own_ref, other_ref)):
                out_ref[
                    at * step * rows : (at + 1) * step * rows,
                    place * columns : (place + 1) * columns,
                ] = product(left, right_ref[...], 1, 1 if turned else 0).astype(jnp.bfloat16)

    return pl.pallas_call(
        kernel,
        grid=(1,),
        in_specs=[
            pl.BlockSpec((count, rows, width), lambda i: (0, 0, 0)),
            pl.BlockSpec(own.shape, lambda i: (0, 0)),
            pl.BlockSpec(other.shape, lambda i: (0, 0)),
        ],
        out_specs=pl.BlockSpec((count * rows, 2 * columns), lambda i: (0, 0)),
        out_shape=jax.ShapeDtypeStruct((count * rows, 2 * columns), jnp.bfloat16),
        compiler_params=pltpu.CompilerParams(vmem_limit_bytes=VMEM),
        cost_estimate=pl.CostEstimate(
            flops=4 * count * rows * width * columns, bytes_accessed=4 << 20, transcendentals=0
        ),
    )(blocks, own, other)


def joined(blocks, own, other, turned):
    count, rows, _ = blocks.shape
    units, width = own.shape[::-1] if turned else own.shape
    step = count // 4

    def kernel(left_ref, own_ref, other_ref, out_ref):
        for at in range(4):
            left = left_ref[at * step : (at + 1) * step].reshape(step * rows, 2 * units)
            dim = 1 if turned else 0
            total = product(left[:, :units], own_ref[...], 1, dim)
            total = total + product(left[:, units:], other_ref[...], 1, dim)
            out_ref[at * step * rows : (at + 1) * step * rows] = total.astype(jnp.bfloat16)

    return pl.pallas_call(
        kernel,
        grid=(1,),
        in_specs=[
            pl.BlockSpec((count, rows, 2 * units), lambda i: (0, 0, 0)),
            pl.BlockSpec(own.shape, lambda i: (0, 0)),
            pl.BlockSpec(other.shape, lambda i: (0, 0)),
        ],
        out_specs=pl.BlockSpec((count * rows, width), lambda i: (0, 0)),
        out_shape=jax.ShapeDtypeStruct((count * rows, width), jnp.bfloat16),
        compiler_params=pltpu.CompilerParams(vmem_limit_bytes=VMEM),
        cost_estimate=pl.CostEstimate(
            flops=4 * count * rows * width * units, bytes_accessed=4 << 20, transcendentals=0
        ),
    )(blocks, own, other)


def packed(pieces, finished, copies):
    count, total_rows, width = pieces.shape
    rows = total_rows // copies

    def kernel(pieces_ref, finished_ref, send_ref):
        for copy in range(copies):
            here = slice(copy * rows, (copy + 1) * rows)
            total = pieces_ref[0, here].astype(jnp.float32)
            for at in range(1, count):
                total = total + pieces_ref[at, here].astype(jnp.float32)
            send_ref[copy, :rows] = finished_ref[here]
            send_ref[copy, rows:] = total.astype(jnp.bfloat16)

    return pl.pallas_call(
        kernel,
        in_specs=[pl.BlockSpec(memory_space=pltpu.VMEM), pl.BlockSpec(memory_space=pltpu.VMEM)],
        out_specs=pl.BlockSpec(memory_space=pltpu.VMEM),
        out_shape=jax.ShapeDtypeStruct((copies, 2 * rows, width), jnp.bfloat16),
    )(pieces, finished)


def cut(value, pieces):
    rows, width = value.shape
    return value.reshape(pieces, rows // pieces, width)


def swapped(value, axis, groups=None):
    return lax.all_to_all(value, axis, 0, 0, axis_index_groups=groups, tiled=True)


def added_up(pieces):
    total = pieces[0].astype(jnp.float32)
    for at in range(1, pieces.shape[0]):
        total = total + pieces[at].astype(jnp.float32)
    return total


def spread(value, axis, size, groups=None):
    return swapped(jnp.broadcast_to(value[None], (size, *value.shape)), axis, groups)


def body(inputs, w_in, w_out, cotangent, counts):
    rows_local = inputs.shape[1]
    width = inputs.shape[2]
    units = w_in.shape[1]
    replicas = lax.axis_size("rep")
    columns = lax.axis_size("col")
    row_count = lax.axis_size("row")
    chips = replicas // CORES
    same_core = [[chip * CORES + core for chip in range(chips)] for core in range(CORES)]
    to_mate = [(r, r // CORES * CORES + (r + 1) % CORES) for r in range(replicas)]
    mate = lambda value: lax.ppermute(value, "rep", to_mate)

    tokens_local = inputs.reshape(rows_local, width)
    send, scaled = prepared(inputs, cotangent, counts, chips)

    w_in_mate, w_out_mate = mate(w_in), mate(w_out)

    line = swapped(send, "rep", same_core)
    tokens_line = line[:, :rows_local].reshape(chips * rows_local, width)
    scaled_line = line[:, rows_local:].reshape(chips * rows_local, width)
    line_rows = chips * rows_local
    rows_all = columns * line_rows

    padded = jnp.concatenate([scaled_line, scaled_line[: line_rows * 3 // 8]], axis=0)
    scaled_blocks = lax.all_gather(padded, "col", axis=0)

    def forward(line):
        blocks = spread(line, "col", columns)
        return blocks, paired(blocks, line_rows, w_in, w_in_mate, False)

    def forward_plain(line):
        blocks = lax.all_gather(line, "col", axis=0)
        return blocks, paired(blocks, line_rows, w_in, w_in_mate, False)

    in_grid = lax.axis_index("col") >= 0
    tokens_blocks, hidden_terms = lax.cond(in_grid, forward_plain, forward, tokens_line)
    slope_terms = paired(scaled_blocks, line_rows, w_out, w_out_mate, True)

    hidden_pieces = swapped(cut(hidden_terms, row_count), "row")
    hidden_pieces, slope_terms = lax.optimization_barrier((hidden_pieces, slope_terms))
    hidden = added_up(hidden_pieces)
    active, slope = gelu_both(hidden)
    share = jnp.broadcast_to(active.astype(jnp.bfloat16)[None], (row_count, *active.shape))
    mixed = swapped(jnp.concatenate([share, cut(slope_terms, row_count)], axis=2), "row")
    activated = mixed[:, :, : active.shape[1]].reshape(rows_all, -1)
    grad_share = (added_up(mixed[:, :, active.shape[1] :]) * slope).astype(jnp.bfloat16)
    output_terms = joined(mixed, w_out, w_out_mate, False)
    output_line = lax.psum_scatter(output_terms, "col", scatter_dimension=0, tiled=True)
    tokens_all = tokens_blocks.reshape(rows_all, width)
    scaled_all = scaled_blocks[:, :line_rows].reshape(rows_all, width)

    def backward(share):
        return backward_parts(spread(share, "row", row_count))

    def backward_plain(share):
        return backward_parts(lax.all_gather(share, "row", axis=0))

    def backward_parts(shares):
        back_terms = joined(shares, w_in, w_in_mate, True)
        hidden_grad = shares.reshape(rows_all, -1)
        back_pieces = swapped(cut(back_terms, columns), "col")
        w_out_grad = product(activated[:, :units], scaled_all, 0, 0) + product(
            mate(activated[:, units:]), mate(scaled_all), 0, 0
        )
        w_in_grad = product(tokens_all, hidden_grad[:, :units], 0, 0) + product(
            mate(tokens_all), mate(hidden_grad[:, units:]), 0, 0
        )
        return back_pieces, w_in_grad, w_out_grad

    back_pieces, w_in_grad, w_out_grad = lax.cond(in_grid, backward, backward_plain, grad_share)
    ends = packed(back_pieces, output_line, chips)
    finished = added_up(swapped(ends, "rep", same_core))
    block_output = (tokens_local.astype(jnp.float32) + finished[:rows_local]).astype(jnp.bfloat16)
    input_grad = (scaled.astype(jnp.float32) + finished[rows_local:]).astype(jnp.bfloat16)

    return (
        block_output.reshape(1, rows_local, width),
        input_grad.reshape(1, rows_local, width),
        w_in_grad,
        w_out_grad,
    )


def solution(mesh):
    placed = (
        P("rep", "col", "row"),
        P("row", ("rep", "col")),
        P(("rep", "col"), "row"),
        P("rep", "col", "row"),
        P(),
    )
    return jax.shard_map(
        body,
        mesh=mesh,
        in_specs=placed,
        out_specs=(
            P("rep", "col", "row"),
            P("rep", "col", "row"),
            P("row", ("rep", "col")),
            P(("rep", "col"), "row"),
        ),
        check_vma=False,
    )
```

```python
import jax
import jax.numpy as jnp
from jax import lax
from jax.experimental import pallas as pl
from jax.experimental.pallas import tpu as pltpu
from jax.sharding import PartitionSpec as P

MBT = 32
CORES = 2
VMEM = 24 << 20

root_coef = 0.7978845608028654
cubic_coef = 0.044715


def gelu_both(values):
    inner = root_coef * (values + cubic_coef * values * values * values)
    tangent = jnp.tanh(inner)
    slope = 0.5 * (1.0 + tangent) + 0.5 * values * (1.0 - tangent * tangent) * root_coef * (
        1.0 + 3.0 * cubic_coef * values * values
    )
    return 0.5 * values * (1.0 + tangent), slope


def product(left, right, left_dim, right_dim):
    return lax.dot_general(
        left, right, (((left_dim,), (right_dim,)), ((), ())), preferred_element_type=jnp.float32
    )


def prepared(tokens, cotangent, counts, copies):
    _, rows, width = tokens.shape

    def kernel(counts_ref, tokens_ref, cotangent_ref, send_ref, scaled_ref):
        own_count = counts_ref[lax.axis_index("rep")]
        total = counts_ref[0]
        for replica in range(1, counts.shape[0]):
            total = total + counts_ref[replica]
        token_total = (MBT * total).astype(jnp.float32)
        positions = lax.axis_index("col") * rows + lax.broadcasted_iota(
            jnp.int32, (rows, width), 0
        )
        kept_mask = (positions < MBT * own_count).astype(jnp.float32)
        scaled = (cotangent_ref[0].astype(jnp.float32) * kept_mask / token_total).astype(
            jnp.bfloat16
        )
        scaled_ref[...] = scaled
        for copy in range(copies):
            send_ref[copy, :rows] = tokens_ref[0]
            send_ref[copy, rows:] = scaled

    return pl.pallas_call(
        kernel,
        in_specs=[
            pl.BlockSpec(memory_space=pltpu.SMEM),
            pl.BlockSpec(memory_space=pltpu.VMEM),
            pl.BlockSpec(memory_space=pltpu.VMEM),
        ],
        out_specs=[pl.BlockSpec(memory_space=pltpu.VMEM), pl.BlockSpec(memory_space=pltpu.VMEM)],
        out_shape=[
            jax.ShapeDtypeStruct((copies, 2 * rows, width), jnp.bfloat16),
            jax.ShapeDtypeStruct((rows, width), jnp.bfloat16),
        ],
    )(counts, tokens, cotangent)


def whole(array):
    return pl.BlockSpec(array.shape, lambda i: (0,) * len(array.shape))


def inward(blocks, w_in, w_in_mate, w_out, w_out_mate):
    places, chips, rows, width = blocks.shape
    rows //= 2
    units = w_in.shape[1]
    step = places // 4
    height = step * chips * rows

    def kernel(blocks_ref, in_ref, in_mate_ref, out_ref, out_mate_ref, terms_ref):
        for at in range(4):
            here = slice(at * step, (at + 1) * step)
            lines = slice(at * height, (at + 1) * height)
            tokens = blocks_ref[here, :, :rows].reshape(height, width)
            scaled = blocks_ref[here, :, rows:].reshape(height, width)
            for place, (left, right, dim) in enumerate(
                (
                    (tokens, in_ref, 0),
                    (tokens, in_mate_ref, 0),
                    (scaled, out_ref, 1),
                    (scaled, out_mate_ref, 1),
                )
            ):
                terms_ref[lines, place * units : (place + 1) * units] = product(
                    left, right[...], 1, dim
                ).astype(jnp.bfloat16)

    total = places * chips * rows
    weights = (w_in, w_in_mate, w_out, w_out_mate)
    return pl.pallas_call(
        kernel,
        grid=(1,),
        in_specs=[whole(blocks)] + [whole(w) for w in weights],
        out_specs=pl.BlockSpec((total, 4 * units), lambda i: (0, 0)),
        out_shape=jax.ShapeDtypeStruct((total, 4 * units), jnp.bfloat16),
        compiler_params=pltpu.CompilerParams(vmem_limit_bytes=VMEM),
        cost_estimate=pl.CostEstimate(
            flops=8 * total * width * units, bytes_accessed=6 << 20, transcendentals=0
        ),
    )(blocks, *weights)


def outward(shares, w_in, w_in_mate, w_out, w_out_mate):
    total = shares.shape[0] * shares.shape[1]
    units = shares.shape[2] // 4
    width = w_in.shape[0]
    step = shares.shape[0] // 4
    height = total // 4

    def kernel(shares_ref, in_ref, in_mate_ref, out_ref, out_mate_ref, terms_ref):
        for at in range(4):
            left = shares_ref[at * step : (at + 1) * step].reshape(height, 4 * units)
            part = [left[:, k * units : (k + 1) * units] for k in range(4)]
            lines = slice(at * height, (at + 1) * height)
            mixed = product(part[0], out_ref[...], 1, 0) + product(part[1], out_mate_ref[...], 1, 0)
            terms_ref[lines, :width] = mixed.astype(jnp.bfloat16)
            back = product(part[2], in_ref[...], 1, 1) + product(part[3], in_mate_ref[...], 1, 1)
            terms_ref[lines, width:] = back.astype(jnp.bfloat16)

    weights = (w_in, w_in_mate, w_out, w_out_mate)
    return pl.pallas_call(
        kernel,
        grid=(1,),
        in_specs=[whole(shares)] + [whole(w) for w in weights],
        out_specs=pl.BlockSpec((total, 2 * width), lambda i: (0, 0)),
        out_shape=jax.ShapeDtypeStruct((total, 2 * width), jnp.bfloat16),
        compiler_params=pltpu.CompilerParams(vmem_limit_bytes=VMEM),
        cost_estimate=pl.CostEstimate(
            flops=8 * total * width * units, bytes_accessed=6 << 20, transcendentals=0
        ),
    )(shares, *weights)


def cut(value, pieces):
    rows, width = value.shape
    return value.reshape(pieces, rows // pieces, width)


def swapped(value, axis, groups=None):
    return lax.all_to_all(value, axis, 0, 0, axis_index_groups=groups, tiled=True)


def added_up(pieces):
    total = pieces[0].astype(jnp.float32)
    for at in range(1, pieces.shape[0]):
        total = total + pieces[at].astype(jnp.float32)
    return total


def spread(value, axis, size, groups=None):
    return swapped(jnp.broadcast_to(value[None], (size, *value.shape)), axis, groups)


def body(inputs, w_in, w_out, cotangent, counts):
    rows_local = inputs.shape[1]
    width = inputs.shape[2]
    units = w_in.shape[1]
    replicas = lax.axis_size("rep")
    columns = lax.axis_size("col")
    row_count = lax.axis_size("row")
    chips = replicas // CORES
    same_core = [[chip * CORES + core for chip in range(chips)] for core in range(CORES)]
    to_mate = [(r, r // CORES * CORES + (r + 1) % CORES) for r in range(replicas)]
    mate = lambda value: lax.ppermute(value, "rep", to_mate)

    tokens_local = inputs.reshape(rows_local, width)
    send, scaled = prepared(inputs, cotangent, counts, chips)

    w_in_mate, w_out_mate = mate(w_in), mate(w_out)

    weights = (w_in, w_in_mate, w_out, w_out_mate)

    rows_all = columns * chips * rows_local
    blocks = spread(swapped(send, "rep", same_core), "col", columns)
    terms = inward(blocks, *weights)
    sums = added_up(swapped(cut(terms, row_count), "row"))
    active, slope = gelu_both(sums[:, : 2 * units])
    share = jnp.concatenate(
        [active.astype(jnp.bfloat16), (sums[:, 2 * units :] * slope).astype(jnp.bfloat16)], axis=1
    )
    shares = spread(share, "row", row_count)
    ends = outward(shares, *weights)
    ends_line = added_up(swapped(cut(ends, columns), "col")).astype(jnp.bfloat16)
    finished = added_up(swapped(cut(ends_line, chips), "rep", same_core))
    block_output = (tokens_local.astype(jnp.float32) + finished[:, :width]).astype(jnp.bfloat16)
    input_grad = (scaled.astype(jnp.float32) + finished[:, width:]).astype(jnp.bfloat16)

    blocks_mate = mate(blocks)
    tokens_all, scaled_all, tokens_mate, scaled_mate = [
        b[:, :, at : at + rows_local].reshape(rows_all, width)
        for b in (blocks, blocks_mate)
        for at in (0, rows_local)
    ]
    shares = shares.reshape(rows_all, 4 * units)
    part = lambda k: shares[:, k * units : (k + 1) * units]
    from_mate = mate(jnp.concatenate([part(1), part(3)], axis=1))
    w_in_grad = product(tokens_all, part(2), 0, 0) + product(
        tokens_mate, from_mate[:, units:], 0, 0
    )
    w_out_grad = product(part(0), scaled_all, 0, 0) + product(
        from_mate[:, :units], scaled_mate, 0, 0
    )
    return (
        block_output.reshape(1, rows_local, width),
        input_grad.reshape(1, rows_local, width),
        w_in_grad,
        w_out_grad,
    )


def solution(mesh):
    placed = (
        P("rep", "col", "row"),
        P("row", ("rep", "col")),
        P(("rep", "col"), "row"),
        P("rep", "col", "row"),
        P(),
    )
    return jax.shard_map(
        body,
        mesh=mesh,
        in_specs=placed,
        out_specs=(
            P("rep", "col", "row"),
            P("rep", "col", "row"),
            P("row", ("rep", "col")),
            P(("rep", "col"), "row"),
        ),
        check_vma=False,
    )
```

```python
import jax
import jax.numpy as jnp
from jax import lax
from jax.experimental import pallas as pl
from jax.experimental.pallas import tpu as pltpu
from jax.sharding import PartitionSpec as P

MBT = 32
CORES = 2
VMEM = 24 << 20

root_coef = 0.7978845608028654
cubic_coef = 0.044715


def gelu_both(values):
    inner = root_coef * (values + cubic_coef * values * values * values)
    tangent = jnp.tanh(inner)
    slope = 0.5 * (1.0 + tangent) + 0.5 * values * (1.0 - tangent * tangent) * root_coef * (
        1.0 + 3.0 * cubic_coef * values * values
    )
    return 0.5 * values * (1.0 + tangent), slope


def product(left, right, left_dim, right_dim):
    return lax.dot_general(
        left, right, (((left_dim,), (right_dim,)), ((), ())), preferred_element_type=jnp.float32
    )


def prepared(tokens, cotangent, counts, copies):
    _, rows, width = tokens.shape

    def kernel(counts_ref, tokens_ref, cotangent_ref, send_ref, scaled_ref):
        own_count = counts_ref[lax.axis_index("rep")]
        total = counts_ref[0]
        for replica in range(1, counts.shape[0]):
            total = total + counts_ref[replica]
        token_total = (MBT * total).astype(jnp.float32)
        positions = lax.axis_index("col") * rows + lax.broadcasted_iota(
            jnp.int32, (rows, width), 0
        )
        kept_mask = (positions < MBT * own_count).astype(jnp.float32)
        scaled = (cotangent_ref[0].astype(jnp.float32) * kept_mask / token_total).astype(
            jnp.bfloat16
        )
        scaled_ref[...] = scaled
        for copy in range(copies):
            send_ref[copy, :rows] = tokens_ref[0]
            send_ref[copy, rows:] = scaled

    return pl.pallas_call(
        kernel,
        in_specs=[
            pl.BlockSpec(memory_space=pltpu.SMEM),
            pl.BlockSpec(memory_space=pltpu.VMEM),
            pl.BlockSpec(memory_space=pltpu.VMEM),
        ],
        out_specs=[pl.BlockSpec(memory_space=pltpu.VMEM), pl.BlockSpec(memory_space=pltpu.VMEM)],
        out_shape=[
            jax.ShapeDtypeStruct((copies, 2 * rows, width), jnp.bfloat16),
            jax.ShapeDtypeStruct((rows, width), jnp.bfloat16),
        ],
    )(counts, tokens, cotangent)


def paired(blocks, rows, own, other, turned):
    count, _, width = blocks.shape
    columns = own.shape[0] if turned else own.shape[1]
    step = count // 4

    def kernel(left_ref, own_ref, other_ref, out_ref):
        for at in range(4):
            left = left_ref[at * step : (at + 1) * step].reshape(step * rows, width)
            for place, right_ref in enumerate((own_ref, other_ref)):
                out_ref[
                    at * step * rows : (at + 1) * step * rows,
                    place * columns : (place + 1) * columns,
                ] = product(left, right_ref[...], 1, 1 if turned else 0).astype(jnp.bfloat16)

    return pl.pallas_call(
        kernel,
        grid=(1,),
        in_specs=[
            pl.BlockSpec((count, rows, width), lambda i: (0, 0, 0)),
            pl.BlockSpec(own.shape, lambda i: (0, 0)),
            pl.BlockSpec(other.shape, lambda i: (0, 0)),
        ],
        out_specs=pl.BlockSpec((count * rows, 2 * columns), lambda i: (0, 0)),
        out_shape=jax.ShapeDtypeStruct((count * rows, 2 * columns), jnp.bfloat16),
        compiler_params=pltpu.CompilerParams(vmem_limit_bytes=VMEM),
        cost_estimate=pl.CostEstimate(
            flops=4 * count * rows * width * columns, bytes_accessed=4 << 20, transcendentals=0
        ),
    )(blocks, own, other)


def joined(blocks, own, other, turned):
    count, rows, _ = blocks.shape
    units, width = own.shape[::-1] if turned else own.shape
    step = count // 4

    def kernel(left_ref, own_ref, other_ref, out_ref):
        for at in range(4):
            left = left_ref[at * step : (at + 1) * step].reshape(step * rows, 2 * units)
            dim = 1 if turned else 0
            total = product(left[:, :units], own_ref[...], 1, dim)
            total = total + product(left[:, units:], other_ref[...], 1, dim)
            out_ref[at * step * rows : (at + 1) * step * rows] = total.astype(jnp.bfloat16)

    return pl.pallas_call(
        kernel,
        grid=(1,),
        in_specs=[
            pl.BlockSpec((count, rows, 2 * units), lambda i: (0, 0, 0)),
            pl.BlockSpec(own.shape, lambda i: (0, 0)),
            pl.BlockSpec(other.shape, lambda i: (0, 0)),
        ],
        out_specs=pl.BlockSpec((count * rows, width), lambda i: (0, 0)),
        out_shape=jax.ShapeDtypeStruct((count * rows, width), jnp.bfloat16),
        compiler_params=pltpu.CompilerParams(vmem_limit_bytes=VMEM),
        cost_estimate=pl.CostEstimate(
            flops=4 * count * rows * width * units, bytes_accessed=4 << 20, transcendentals=0
        ),
    )(blocks, own, other)


def cut(value, pieces):
    rows, width = value.shape
    return value.reshape(pieces, rows // pieces, width)


def swapped(value, axis, groups=None):
    return lax.all_to_all(value, axis, 0, 0, axis_index_groups=groups, tiled=True)


def added_up(pieces):
    total = pieces[0].astype(jnp.float32)
    for at in range(1, pieces.shape[0]):
        total = total + pieces[at].astype(jnp.float32)
    return total


def spread(value, axis, size, groups=None):
    return swapped(jnp.broadcast_to(value[None], (size, *value.shape)), axis, groups)


def body(inputs, w_in, w_out, cotangent, counts):
    rows_local = inputs.shape[1]
    width = inputs.shape[2]
    units = w_in.shape[1]
    replicas = lax.axis_size("rep")
    columns = lax.axis_size("col")
    row_count = lax.axis_size("row")
    chips = replicas // CORES
    same_core = [[chip * CORES + core for chip in range(chips)] for core in range(CORES)]
    to_mate = [(r, r // CORES * CORES + (r + 1) % CORES) for r in range(replicas)]
    mate = lambda value: lax.ppermute(value, "rep", to_mate)

    tokens_local = inputs.reshape(rows_local, width)
    send, scaled = prepared(inputs, cotangent, counts, chips)

    w_in_mate, w_out_mate = mate(w_in), mate(w_out)

    line = swapped(send, "rep", same_core)
    tokens_line = line[:, :rows_local].reshape(chips * rows_local, width)
    scaled_line = line[:, rows_local:].reshape(chips * rows_local, width)
    line_rows = chips * rows_local
    rows_all = columns * line_rows

    tokens_blocks = lax.all_gather(tokens_line, "col", axis=0)
    hidden_terms = paired(tokens_blocks, line_rows, w_in, w_in_mate, False)
    hidden_terms, scaled_line = lax.optimization_barrier((hidden_terms, scaled_line))
    scaled_blocks = lax.all_gather(scaled_line, "col", axis=0)
    slope_terms = paired(scaled_blocks, line_rows, w_out, w_out_mate, True)
    hidden_pieces = swapped(cut(hidden_terms, row_count), "row")
    hidden_pieces, slope_terms = lax.optimization_barrier((hidden_pieces, slope_terms))

    hidden = added_up(hidden_pieces)
    active, slope = gelu_both(hidden)
    share = jnp.broadcast_to(active.astype(jnp.bfloat16)[None], (row_count, *active.shape))
    mixed = swapped(jnp.concatenate([share, cut(slope_terms, row_count)], axis=2), "row")
    activated = mixed[:, :, : active.shape[1]].reshape(rows_all, -1)
    grad_share = (added_up(mixed[:, :, active.shape[1] :]) * slope).astype(jnp.bfloat16)
    output_terms = joined(mixed, w_out, w_out_mate, False)
    tokens_all = tokens_blocks.reshape(rows_all, width)
    scaled_all = scaled_blocks[:, :line_rows].reshape(rows_all, width)

    shares = spread(grad_share, "row", row_count)
    back_terms = joined(shares, w_in, w_in_mate, True)
    hidden_grad = shares.reshape(rows_all, -1)
    ends = jnp.concatenate([output_terms, back_terms], axis=1)
    ends_line = added_up(swapped(cut(ends, columns), "col")).astype(jnp.bfloat16)
    finished = added_up(swapped(cut(ends_line, chips), "rep", same_core))
    block_output = (tokens_local.astype(jnp.float32) + finished[:, :width]).astype(jnp.bfloat16)
    input_grad = (scaled.astype(jnp.float32) + finished[:, width:]).astype(jnp.bfloat16)

    w_out_grad = product(activated[:, :units], scaled_all, 0, 0) + product(
        mate(activated[:, units:]), mate(scaled_all), 0, 0
    )
    w_in_grad = product(tokens_all, hidden_grad[:, :units], 0, 0) + product(
        mate(tokens_all), mate(hidden_grad[:, units:]), 0, 0
    )
    return (
        block_output.reshape(1, rows_local, width),
        input_grad.reshape(1, rows_local, width),
        w_in_grad,
        w_out_grad,
    )


def solution(mesh):
    placed = (
        P("rep", "col", "row"),
        P("row", ("rep", "col")),
        P(("rep", "col"), "row"),
        P("rep", "col", "row"),
        P(),
    )
    return jax.shard_map(
        body,
        mesh=mesh,
        in_specs=placed,
        out_specs=(
            P("rep", "col", "row"),
            P("rep", "col", "row"),
            P("row", ("rep", "col")),
            P(("rep", "col"), "row"),
        ),
        check_vma=False,
    )
```

```python
import jax
import jax.numpy as jnp
from jax import lax
from jax.experimental import pallas as pl
from jax.experimental.pallas import tpu as pltpu
from jax.sharding import PartitionSpec as P

MBT = 32
CORES = 2
VMEM = 24 << 20

root_coef = 0.7978845608028654
cubic_coef = 0.044715


def gelu_both(values):
    inner = root_coef * (values + cubic_coef * values * values * values)
    tangent = jnp.tanh(inner)
    slope = 0.5 * (1.0 + tangent) + 0.5 * values * (1.0 - tangent * tangent) * root_coef * (
        1.0 + 3.0 * cubic_coef * values * values
    )
    return 0.5 * values * (1.0 + tangent), slope


def product(left, right, left_dim, right_dim):
    return lax.dot_general(
        left, right, (((left_dim,), (right_dim,)), ((), ())), preferred_element_type=jnp.float32
    )


def prepared(tokens, cotangent, counts, copies):
    _, rows, width = tokens.shape

    def kernel(counts_ref, tokens_ref, cotangent_ref, send_ref, scaled_ref):
        own_count = counts_ref[lax.axis_index("rep")]
        total = counts_ref[0]
        for replica in range(1, counts.shape[0]):
            total = total + counts_ref[replica]
        token_total = (MBT * total).astype(jnp.float32)
        positions = lax.axis_index("col") * rows + lax.broadcasted_iota(
            jnp.int32, (rows, width), 0
        )
        kept_mask = (positions < MBT * own_count).astype(jnp.float32)
        scaled = (cotangent_ref[0].astype(jnp.float32) * kept_mask / token_total).astype(
            jnp.bfloat16
        )
        scaled_ref[...] = scaled
        for copy in range(copies):
            send_ref[copy, :rows] = tokens_ref[0]
            send_ref[copy, rows:] = scaled

    return pl.pallas_call(
        kernel,
        in_specs=[
            pl.BlockSpec(memory_space=pltpu.SMEM),
            pl.BlockSpec(memory_space=pltpu.VMEM),
            pl.BlockSpec(memory_space=pltpu.VMEM),
        ],
        out_specs=[pl.BlockSpec(memory_space=pltpu.VMEM), pl.BlockSpec(memory_space=pltpu.VMEM)],
        out_shape=[
            jax.ShapeDtypeStruct((copies, 2 * rows, width), jnp.bfloat16),
            jax.ShapeDtypeStruct((rows, width), jnp.bfloat16),
        ],
    )(counts, tokens, cotangent)


def paired(blocks, rows, own, other, turned):
    count, _, width = blocks.shape
    columns = own.shape[0] if turned else own.shape[1]
    step = count // 4

    def kernel(left_ref, own_ref, other_ref, out_ref):
        for at in range(4):
            left = left_ref[at * step : (at + 1) * step].reshape(step * rows, width)
            for place, right_ref in enumerate((own_ref, other_ref)):
                out_ref[
                    at * step * rows : (at + 1) * step * rows,
                    place * columns : (place + 1) * columns,
                ] = product(left, right_ref[...], 1, 1 if turned else 0).astype(jnp.bfloat16)

    return pl.pallas_call(
        kernel,
        grid=(1,),
        in_specs=[
            pl.BlockSpec((count, rows, width), lambda i: (0, 0, 0)),
            pl.BlockSpec(own.shape, lambda i: (0, 0)),
            pl.BlockSpec(other.shape, lambda i: (0, 0)),
        ],
        out_specs=pl.BlockSpec((count * rows, 2 * columns), lambda i: (0, 0)),
        out_shape=jax.ShapeDtypeStruct((count * rows, 2 * columns), jnp.bfloat16),
        compiler_params=pltpu.CompilerParams(vmem_limit_bytes=VMEM),
        cost_estimate=pl.CostEstimate(
            flops=4 * count * rows * width * columns, bytes_accessed=4 << 20, transcendentals=0
        ),
    )(blocks, own, other)


def joined(blocks, own, other, turned):
    count, rows, _ = blocks.shape
    units, width = own.shape[::-1] if turned else own.shape
    step = count // 4

    def kernel(left_ref, own_ref, other_ref, out_ref):
        for at in range(4):
            left = left_ref[at * step : (at + 1) * step].reshape(step * rows, 2 * units)
            dim = 1 if turned else 0
            total = product(left[:, :units], own_ref[...], 1, dim)
            total = total + product(left[:, units:], other_ref[...], 1, dim)
            out_ref[at * step * rows : (at + 1) * step * rows] = total.astype(jnp.bfloat16)

    return pl.pallas_call(
        kernel,
        grid=(1,),
        in_specs=[
            pl.BlockSpec((count, rows, 2 * units), lambda i: (0, 0, 0)),
            pl.BlockSpec(own.shape, lambda i: (0, 0)),
            pl.BlockSpec(other.shape, lambda i: (0, 0)),
        ],
        out_specs=pl.BlockSpec((count * rows, width), lambda i: (0, 0)),
        out_shape=jax.ShapeDtypeStruct((count * rows, width), jnp.bfloat16),
        compiler_params=pltpu.CompilerParams(vmem_limit_bytes=VMEM),
        cost_estimate=pl.CostEstimate(
            flops=4 * count * rows * width * units, bytes_accessed=4 << 20, transcendentals=0
        ),
    )(blocks, own, other)


def cut(value, pieces):
    rows, width = value.shape
    return value.reshape(pieces, rows // pieces, width)


def swapped(value, axis, groups=None):
    return lax.all_to_all(value, axis, 0, 0, axis_index_groups=groups, tiled=True)


def added_up(pieces):
    total = pieces[0].astype(jnp.float32)
    for at in range(1, pieces.shape[0]):
        total = total + pieces[at].astype(jnp.float32)
    return total


def spread(value, axis, size, groups=None):
    return swapped(jnp.broadcast_to(value[None], (size, *value.shape)), axis, groups)


def body(inputs, w_in, w_out, cotangent, counts):
    rows_local = inputs.shape[1]
    width = inputs.shape[2]
    units = w_in.shape[1]
    replicas = lax.axis_size("rep")
    columns = lax.axis_size("col")
    row_count = lax.axis_size("row")
    chips = replicas // CORES
    same_core = [[chip * CORES + core for chip in range(chips)] for core in range(CORES)]
    to_mate = [(r, r // CORES * CORES + (r + 1) % CORES) for r in range(replicas)]
    mate = lambda value: lax.ppermute(value, "rep", to_mate)

    tokens_local = inputs.reshape(rows_local, width)
    send, scaled = prepared(inputs, cotangent, counts, chips)

    w_in_mate, w_out_mate = mate(w_in), mate(w_out)

    line = swapped(send, "rep", same_core)
    tokens_line = line[:, :rows_local].reshape(chips * rows_local, width)
    scaled_line = line[:, rows_local:].reshape(chips * rows_local, width)
    line_rows = chips * rows_local
    rows_all = columns * line_rows

    padded = jnp.concatenate([scaled_line, scaled_line[: line_rows * 3 // 8]], axis=0)
    scaled_blocks = lax.all_gather(padded, "col", axis=0)

    def forward(line):
        blocks = spread(line, "col", columns)
        return blocks, paired(blocks, line_rows, w_in, w_in_mate, False)

    def forward_plain(line):
        blocks = lax.all_gather(line, "col", axis=0)
        return blocks, paired(blocks, line_rows, w_in, w_in_mate, False)

    in_grid = lax.axis_index("col") >= 0
    tokens_blocks, hidden_terms = lax.cond(in_grid, forward_plain, forward, tokens_line)
    slope_terms = paired(scaled_blocks, line_rows, w_out, w_out_mate, True)

    hidden_pieces = swapped(cut(hidden_terms, row_count), "row")
    hidden_pieces, slope_terms = lax.optimization_barrier((hidden_pieces, slope_terms))
    hidden = added_up(hidden_pieces)
    active, slope = gelu_both(hidden)
    share = jnp.broadcast_to(active.astype(jnp.bfloat16)[None], (row_count, *active.shape))
    mixed = swapped(jnp.concatenate([share, cut(slope_terms, row_count)], axis=2), "row")
    activated = mixed[:, :, : active.shape[1]].reshape(rows_all, -1)
    grad_share = (added_up(mixed[:, :, active.shape[1] :]) * slope).astype(jnp.bfloat16)
    output_terms = joined(mixed, w_out, w_out_mate, False)
    output_line = lax.psum_scatter(output_terms, "col", scatter_dimension=0, tiled=True)
    tokens_all = tokens_blocks.reshape(rows_all, width)
    scaled_all = scaled_blocks[:, :line_rows].reshape(rows_all, width)

    def backward(share):
        shares = spread(share, "row", row_count)
        w_out_grad = product(activated[:, :units], scaled_all, 0, 0) + product(
            mate(activated[:, units:]), mate(scaled_all), 0, 0
        )
        return *backward_parts(shares), w_out_grad

    def backward_plain(share):
        shares = lax.all_gather(share, "row", axis=0)
        full = product(mixed.reshape(rows_all, 4 * units), scaled_all, 0, 0)
        return *backward_parts(shares), full[:units] + mate(full[units : 2 * units])

    def backward_parts(shares):
        back_terms = joined(shares, w_in, w_in_mate, True)
        hidden_grad = shares.reshape(rows_all, -1)
        back_line = added_up(swapped(cut(back_terms, columns), "col")).astype(jnp.bfloat16)
        w_in_grad = product(tokens_all, hidden_grad[:, :units], 0, 0) + product(
            mate(tokens_all), mate(hidden_grad[:, units:]), 0, 0
        )
        return back_line, w_in_grad

    back_line, w_in_grad, w_out_grad = lax.cond(in_grid, backward, backward_plain, grad_share)
    ends = jnp.concatenate([cut(output_line, chips), cut(back_line, chips)], axis=1)
    finished = added_up(swapped(ends, "rep", same_core))
    block_output = (tokens_local.astype(jnp.float32) + finished[:rows_local]).astype(jnp.bfloat16)
    input_grad = (scaled.astype(jnp.float32) + finished[rows_local:]).astype(jnp.bfloat16)

    return (
        block_output.reshape(1, rows_local, width),
        input_grad.reshape(1, rows_local, width),
        w_in_grad,
        w_out_grad,
    )


def solution(mesh):
    placed = (
        P("rep", "col", "row"),
        P("row", ("rep", "col")),
        P(("rep", "col"), "row"),
        P("rep", "col", "row"),
        P(),
    )
    return jax.shard_map(
        body,
        mesh=mesh,
        in_specs=placed,
        out_specs=(
            P("rep", "col", "row"),
            P("rep", "col", "row"),
            P("row", ("rep", "col")),
            P(("rep", "col"), "row"),
        ),
        check_vma=False,
    )
```

```python
import jax
import jax.numpy as jnp
from jax import lax
from jax.experimental import pallas as pl
from jax.experimental.pallas import tpu as pltpu
from jax.sharding import PartitionSpec as P

MBT = 32
CORES = 2
VMEM = 24 << 20

root_coef = 0.7978845608028654
cubic_coef = 0.044715


def gelu_both(values):
    inner = root_coef * (values + cubic_coef * values * values * values)
    tangent = jnp.tanh(inner)
    slope = 0.5 * (1.0 + tangent) + 0.5 * values * (1.0 - tangent * tangent) * root_coef * (
        1.0 + 3.0 * cubic_coef * values * values
    )
    return 0.5 * values * (1.0 + tangent), slope


def product(left, right, left_dim, right_dim):
    return lax.dot_general(
        left, right, (((left_dim,), (right_dim,)), ((), ())), preferred_element_type=jnp.float32
    )


def prepared(tokens, cotangent, counts, copies):
    _, rows, width = tokens.shape

    def kernel(counts_ref, tokens_ref, cotangent_ref, send_ref, scaled_ref):
        own_count = counts_ref[lax.axis_index("rep")]
        total = counts_ref[0]
        for replica in range(1, counts.shape[0]):
            total = total + counts_ref[replica]
        token_total = (MBT * total).astype(jnp.float32)
        positions = lax.axis_index("col") * rows + lax.broadcasted_iota(
            jnp.int32, (rows, width), 0
        )
        kept_mask = (positions < MBT * own_count).astype(jnp.float32)
        scaled = (cotangent_ref[0].astype(jnp.float32) * kept_mask / token_total).astype(
            jnp.bfloat16
        )
        scaled_ref[...] = scaled
        for copy in range(copies):
            send_ref[copy, :rows] = tokens_ref[0]
            send_ref[copy, rows:] = scaled

    return pl.pallas_call(
        kernel,
        in_specs=[
            pl.BlockSpec(memory_space=pltpu.SMEM),
            pl.BlockSpec(memory_space=pltpu.VMEM),
            pl.BlockSpec(memory_space=pltpu.VMEM),
        ],
        out_specs=[pl.BlockSpec(memory_space=pltpu.VMEM), pl.BlockSpec(memory_space=pltpu.VMEM)],
        out_shape=[
            jax.ShapeDtypeStruct((copies, 2 * rows, width), jnp.bfloat16),
            jax.ShapeDtypeStruct((rows, width), jnp.bfloat16),
        ],
    )(counts, tokens, cotangent)


def paired(blocks, rows, own, other, turned, parts):
    count, _, width = blocks.shape
    columns = own.shape[0] if turned else own.shape[1]
    step = count // 4

    def kernel(left_ref, own_ref, other_ref, out_ref):
        for at in range(4 // parts):
            left = left_ref[at * step : (at + 1) * step].reshape(step * rows, width)
            for place, right_ref in enumerate((own_ref, other_ref)):
                out_ref[
                    at * step * rows : (at + 1) * step * rows,
                    place * columns : (place + 1) * columns,
                ] = product(left, right_ref[...], 1, 1 if turned else 0).astype(jnp.bfloat16)

    return pl.pallas_call(
        kernel,
        grid=(parts,),
        in_specs=[
            pl.BlockSpec((count // parts, rows, width), lambda i: (i, 0, 0)),
            pl.BlockSpec(own.shape, lambda i: (0, 0)),
            pl.BlockSpec(other.shape, lambda i: (0, 0)),
        ],
        out_specs=pl.BlockSpec((count * rows // parts, 2 * columns), lambda i: (i, 0)),
        out_shape=jax.ShapeDtypeStruct((count * rows, 2 * columns), jnp.bfloat16),
        compiler_params=pltpu.CompilerParams(vmem_limit_bytes=VMEM),
        cost_estimate=pl.CostEstimate(
            flops=4 * count * rows * width * columns, bytes_accessed=4 << 20, transcendentals=0
        ),
    )(blocks, own, other)


def joined(blocks, own, other, turned, parts):
    count, rows, _ = blocks.shape
    units, width = own.shape[::-1] if turned else own.shape
    step = count // 4

    def kernel(left_ref, own_ref, other_ref, out_ref):
        for at in range(4 // parts):
            left = left_ref[at * step : (at + 1) * step].reshape(step * rows, 2 * units)
            dim = 1 if turned else 0
            total = product(left[:, :units], own_ref[...], 1, dim)
            total = total + product(left[:, units:], other_ref[...], 1, dim)
            out_ref[at * step * rows : (at + 1) * step * rows] = total.astype(jnp.bfloat16)

    return pl.pallas_call(
        kernel,
        grid=(parts,),
        in_specs=[
            pl.BlockSpec((count // parts, rows, 2 * units), lambda i: (i, 0, 0)),
            pl.BlockSpec(own.shape, lambda i: (0, 0)),
            pl.BlockSpec(other.shape, lambda i: (0, 0)),
        ],
        out_specs=pl.BlockSpec((count * rows // parts, width), lambda i: (i, 0)),
        out_shape=jax.ShapeDtypeStruct((count * rows, width), jnp.bfloat16),
        compiler_params=pltpu.CompilerParams(vmem_limit_bytes=VMEM),
        cost_estimate=pl.CostEstimate(
            flops=4 * count * rows * width * units, bytes_accessed=4 << 20, transcendentals=0
        ),
    )(blocks, own, other)


def cut(value, pieces):
    rows, width = value.shape
    return value.reshape(pieces, rows // pieces, width)


def swapped(value, axis, groups=None):
    return lax.all_to_all(value, axis, 0, 0, axis_index_groups=groups, tiled=True)


def added_up(pieces):
    total = pieces[0].astype(jnp.float32)
    for at in range(1, pieces.shape[0]):
        total = total + pieces[at].astype(jnp.float32)
    return total


def spread(value, axis, size, groups=None):
    return swapped(jnp.broadcast_to(value[None], (size, *value.shape)), axis, groups)


def body(inputs, w_in, w_out, cotangent, counts):
    rows_local = inputs.shape[1]
    width = inputs.shape[2]
    units = w_in.shape[1]
    replicas = lax.axis_size("rep")
    columns = lax.axis_size("col")
    row_count = lax.axis_size("row")
    chips = replicas // CORES
    same_core = [[chip * CORES + core for chip in range(chips)] for core in range(CORES)]
    to_mate = [(r, r // CORES * CORES + (r + 1) % CORES) for r in range(replicas)]
    mate = lambda value: lax.ppermute(value, "rep", to_mate)

    tokens_local = inputs.reshape(rows_local, width)
    send, scaled = prepared(inputs, cotangent, counts, chips)

    w_in_mate, w_out_mate = mate(w_in), mate(w_out)

    line = swapped(send, "rep", same_core)
    tokens_line = line[:, :rows_local].reshape(chips * rows_local, width)
    scaled_line = line[:, rows_local:].reshape(chips * rows_local, width)
    line_rows = chips * rows_local
    rows_all = columns * line_rows

    padded = jnp.concatenate([scaled_line, scaled_line[: line_rows * 3 // 8]], axis=0)
    scaled_blocks = lax.all_gather(padded, "col", axis=0)

    def forward(line):
        blocks = spread(line, "col", columns)
        return blocks, paired(blocks, line_rows, w_in, w_in_mate, False, 4)

    def forward_plain(line):
        blocks = lax.all_gather(line, "col", axis=0)
        return blocks, paired(blocks, line_rows, w_in, w_in_mate, False, 4)

    in_grid = lax.axis_index("col") >= 0
    tokens_blocks, hidden_terms = lax.cond(in_grid, forward_plain, forward, tokens_line)
    slope_terms = paired(scaled_blocks, line_rows, w_out, w_out_mate, True, 1)

    hidden_pieces = swapped(cut(hidden_terms, row_count), "row")
    hidden_pieces, slope_terms = lax.optimization_barrier((hidden_pieces, slope_terms))
    hidden = added_up(hidden_pieces)
    active, slope = gelu_both(hidden)
    share = jnp.broadcast_to(active.astype(jnp.bfloat16)[None], (row_count, *active.shape))
    mixed = swapped(jnp.concatenate([share, cut(slope_terms, row_count)], axis=2), "row")
    activated = mixed[:, :, : active.shape[1]].reshape(rows_all, -1)
    grad_share = (added_up(mixed[:, :, active.shape[1] :]) * slope).astype(jnp.bfloat16)
    output_terms = joined(mixed, w_out, w_out_mate, False, 1)
    output_line = lax.psum_scatter(output_terms, "col", scatter_dimension=0, tiled=True)
    tokens_all = tokens_blocks.reshape(rows_all, width)
    scaled_all = scaled_blocks[:, :line_rows].reshape(rows_all, width)

    def backward(share):
        shares = spread(share, "row", row_count)
        w_out_grad = product(activated[:, :units], scaled_all, 0, 0) + product(
            mate(activated[:, units:]), mate(scaled_all), 0, 0
        )
        return *backward_parts(shares), w_out_grad

    def backward_plain(share):
        shares = lax.all_gather(share, "row", axis=0)
        full = product(mixed.reshape(rows_all, 4 * units), scaled_all, 0, 0)
        return *backward_parts(shares), full[:units] + mate(full[units : 2 * units])

    def backward_parts(shares):
        back_terms = joined(shares, w_in, w_in_mate, True, 4)
        hidden_grad = shares.reshape(rows_all, -1)
        back_line = added_up(swapped(cut(back_terms, columns), "col")).astype(jnp.bfloat16)
        w_in_grad = product(tokens_all, hidden_grad[:, :units], 0, 0) + product(
            mate(tokens_all), mate(hidden_grad[:, units:]), 0, 0
        )
        return back_line, w_in_grad

    back_line, w_in_grad, w_out_grad = lax.cond(in_grid, backward, backward_plain, grad_share)
    ends = jnp.concatenate([cut(output_line, chips), cut(back_line, chips)], axis=1)
    finished = added_up(swapped(ends, "rep", same_core))
    block_output = (tokens_local.astype(jnp.float32) + finished[:rows_local]).astype(jnp.bfloat16)
    input_grad = (scaled.astype(jnp.float32) + finished[rows_local:]).astype(jnp.bfloat16)

    return (
        block_output.reshape(1, rows_local, width),
        input_grad.reshape(1, rows_local, width),
        w_in_grad,
        w_out_grad,
    )


def solution(mesh):
    placed = (
        P("rep", "col", "row"),
        P("row", ("rep", "col")),
        P(("rep", "col"), "row"),
        P("rep", "col", "row"),
        P(),
    )
    return jax.shard_map(
        body,
        mesh=mesh,
        in_specs=placed,
        out_specs=(
            P("rep", "col", "row"),
            P("rep", "col", "row"),
            P("row", ("rep", "col")),
            P(("rep", "col"), "row"),
        ),
        check_vma=False,
    )
```

```python
import jax
import jax.numpy as jnp
from jax import lax
from jax.experimental import pallas as pl
from jax.experimental.pallas import tpu as pltpu
from jax.sharding import PartitionSpec as P

MBT = 32
CORES = 2
VMEM = 24 << 20

root_coef = 0.7978845608028654
cubic_coef = 0.044715


def gelu_both(values):
    inner = root_coef * (values + cubic_coef * values * values * values)
    tangent = jnp.tanh(inner)
    slope = 0.5 * (1.0 + tangent) + 0.5 * values * (1.0 - tangent * tangent) * root_coef * (
        1.0 + 3.0 * cubic_coef * values * values
    )
    return 0.5 * values * (1.0 + tangent), slope


def product(left, right, left_dim, right_dim):
    return lax.dot_general(
        left, right, (((left_dim,), (right_dim,)), ((), ())), preferred_element_type=jnp.float32
    )


def prepared(tokens, cotangent, counts, copies):
    _, rows, width = tokens.shape

    def kernel(counts_ref, tokens_ref, cotangent_ref, send_ref, scaled_ref):
        own_count = counts_ref[lax.axis_index("rep")]
        total = counts_ref[0]
        for replica in range(1, counts.shape[0]):
            total = total + counts_ref[replica]
        token_total = (MBT * total).astype(jnp.float32)
        positions = lax.axis_index("col") * rows + lax.broadcasted_iota(
            jnp.int32, (rows, width), 0
        )
        kept_mask = (positions < MBT * own_count).astype(jnp.float32)
        scaled = (cotangent_ref[0].astype(jnp.float32) * kept_mask / token_total).astype(
            jnp.bfloat16
        )
        scaled_ref[...] = scaled
        for copy in range(copies):
            send_ref[copy, :rows] = tokens_ref[0]
            send_ref[copy, rows:] = scaled

    return pl.pallas_call(
        kernel,
        in_specs=[
            pl.BlockSpec(memory_space=pltpu.SMEM),
            pl.BlockSpec(memory_space=pltpu.VMEM),
            pl.BlockSpec(memory_space=pltpu.VMEM),
        ],
        out_specs=[pl.BlockSpec(memory_space=pltpu.VMEM), pl.BlockSpec(memory_space=pltpu.VMEM)],
        out_shape=[
            jax.ShapeDtypeStruct((copies, 2 * rows, width), jnp.bfloat16),
            jax.ShapeDtypeStruct((rows, width), jnp.bfloat16),
        ],
    )(counts, tokens, cotangent)


def paired(blocks, rows, own, other, turned):
    count, _, width = blocks.shape
    columns = own.shape[0] if turned else own.shape[1]
    step = count // 4

    def kernel(left_ref, own_ref, other_ref, out_ref):
        for at in range(4):
            left = left_ref[at * step : (at + 1) * step].reshape(step * rows, width)
            for place, right_ref in enumerate((own_ref, other_ref)):
                out_ref[
                    at * step * rows : (at + 1) * step * rows,
                    place * columns : (place + 1) * columns,
                ] = product(left, right_ref[...], 1, 1 if turned else 0).astype(jnp.bfloat16)

    return pl.pallas_call(
        kernel,
        grid=(1,),
        in_specs=[
            pl.BlockSpec((count, rows, width), lambda i: (0, 0, 0)),
            pl.BlockSpec(own.shape, lambda i: (0, 0)),
            pl.BlockSpec(other.shape, lambda i: (0, 0)),
        ],
        out_specs=pl.BlockSpec((count * rows, 2 * columns), lambda i: (0, 0)),
        out_shape=jax.ShapeDtypeStruct((count * rows, 2 * columns), jnp.bfloat16),
        compiler_params=pltpu.CompilerParams(vmem_limit_bytes=VMEM),
        cost_estimate=pl.CostEstimate(
            flops=4 * count * rows * width * columns, bytes_accessed=4 << 20, transcendentals=0
        ),
    )(blocks, own, other)


def joined(blocks, own, other, turned):
    count, rows, _ = blocks.shape
    units, width = own.shape[::-1] if turned else own.shape
    step = count // 4

    def kernel(left_ref, own_ref, other_ref, out_ref):
        for at in range(4):
            left = left_ref[at * step : (at + 1) * step].reshape(step * rows, 2 * units)
            dim = 1 if turned else 0
            total = product(left[:, :units], own_ref[...], 1, dim)
            total = total + product(left[:, units:], other_ref[...], 1, dim)
            out_ref[at * step * rows : (at + 1) * step * rows] = total.astype(jnp.bfloat16)

    return pl.pallas_call(
        kernel,
        grid=(1,),
        in_specs=[
            pl.BlockSpec((count, rows, 2 * units), lambda i: (0, 0, 0)),
            pl.BlockSpec(own.shape, lambda i: (0, 0)),
            pl.BlockSpec(other.shape, lambda i: (0, 0)),
        ],
        out_specs=pl.BlockSpec((count * rows, width), lambda i: (0, 0)),
        out_shape=jax.ShapeDtypeStruct((count * rows, width), jnp.bfloat16),
        compiler_params=pltpu.CompilerParams(vmem_limit_bytes=VMEM),
        cost_estimate=pl.CostEstimate(
            flops=4 * count * rows * width * units, bytes_accessed=4 << 20, transcendentals=0
        ),
    )(blocks, own, other)


def cut(value, pieces):
    rows, width = value.shape
    return value.reshape(pieces, rows // pieces, width)


def swapped(value, axis, groups=None):
    return lax.all_to_all(value, axis, 0, 0, axis_index_groups=groups, tiled=True)


def added_up(pieces):
    total = pieces[0].astype(jnp.float32)
    for at in range(1, pieces.shape[0]):
        total = total + pieces[at].astype(jnp.float32)
    return total


def spread(value, axis, size, groups=None):
    return swapped(jnp.broadcast_to(value[None], (size, *value.shape)), axis, groups)


def body(inputs, w_in, w_out, cotangent, counts):
    rows_local = inputs.shape[1]
    width = inputs.shape[2]
    units = w_in.shape[1]
    replicas = lax.axis_size("rep")
    columns = lax.axis_size("col")
    row_count = lax.axis_size("row")
    chips = replicas // CORES
    same_core = [[chip * CORES + core for chip in range(chips)] for core in range(CORES)]
    to_mate = [(r, r // CORES * CORES + (r + 1) % CORES) for r in range(replicas)]
    mate = lambda value: lax.ppermute(value, "rep", to_mate)

    tokens_local = inputs.reshape(rows_local, width)
    send, scaled = prepared(inputs, cotangent, counts, chips)

    w_in_mate, w_out_mate = mate(w_in), mate(w_out)

    line = swapped(send, "rep", same_core)
    tokens_line = line[:, :rows_local].reshape(chips * rows_local, width)
    scaled_line = line[:, rows_local:].reshape(chips * rows_local, width)
    line_rows = chips * rows_local
    rows_all = columns * line_rows

    padded = jnp.concatenate([scaled_line, scaled_line[: line_rows * 3 // 8]], axis=0)
    scaled_blocks = lax.all_gather(padded, "col", axis=0)

    def forward(line):
        blocks = spread(line, "col", columns)
        return blocks, paired(blocks, line_rows, w_in, w_in_mate, False)

    def forward_plain(line):
        blocks = lax.all_gather(line, "col", axis=0)
        return blocks, paired(blocks, line_rows, w_in, w_in_mate, False)

    in_grid = lax.axis_index("col") >= 0
    tokens_blocks, hidden_terms = lax.cond(in_grid, forward_plain, forward, tokens_line)
    slope_terms = paired(scaled_blocks, line_rows, w_out, w_out_mate, True)

    hidden_pieces = swapped(cut(hidden_terms, row_count), "row")
    hidden_pieces, slope_terms = lax.optimization_barrier((hidden_pieces, slope_terms))
    hidden = added_up(hidden_pieces)
    active, slope = gelu_both(hidden)
    share = jnp.broadcast_to(active.astype(jnp.bfloat16)[None], (row_count, *active.shape))
    mixed = swapped(jnp.concatenate([share, cut(slope_terms, row_count)], axis=2), "row")
    activated = mixed[:, :, : active.shape[1]].reshape(rows_all, -1)
    grad_share = (added_up(mixed[:, :, active.shape[1] :]) * slope).astype(jnp.bfloat16)
    output_terms = joined(mixed, w_out, w_out_mate, False)
    output_line = lax.psum_scatter(output_terms, "col", scatter_dimension=0, tiled=True)
    tokens_all = tokens_blocks.reshape(rows_all, width)
    scaled_all = scaled_blocks[:, :line_rows].reshape(rows_all, width)

    shares = spread(grad_share, "row", row_count)

    def backward(shares):
        w_out_grad = product(activated[:, :units], scaled_all, 0, 0) + product(
            mate(activated[:, units:]), mate(scaled_all), 0, 0
        )
        back_terms = joined(shares, w_in, w_in_mate, True)
        back_pieces = swapped(cut(back_terms, columns), "col")
        return *backward_parts(shares, back_pieces), w_out_grad

    def backward_plain(shares):
        full = product(mixed.reshape(rows_all, 4 * units), scaled_all, 0, 0)
        back_terms = joined(shares, w_in, w_in_mate, True)
        back_pieces = swapped(cut(back_terms, columns), "col")
        return *backward_parts(shares, back_pieces), full[:units] + mate(full[units : 2 * units])

    def backward_parts(shares, back_pieces):
        hidden_grad = shares.reshape(rows_all, -1)
        back_line = added_up(back_pieces).astype(jnp.bfloat16)
        w_in_grad = product(tokens_all, hidden_grad[:, :units], 0, 0) + product(
            mate(tokens_all), mate(hidden_grad[:, units:]), 0, 0
        )
        return back_line, w_in_grad

    back_line, w_in_grad, w_out_grad = lax.cond(in_grid, backward, backward_plain, shares)
    ends = jnp.concatenate([cut(output_line, chips), cut(back_line, chips)], axis=1)
    finished = added_up(swapped(ends, "rep", same_core))
    block_output = (tokens_local.astype(jnp.float32) + finished[:rows_local]).astype(jnp.bfloat16)
    input_grad = (scaled.astype(jnp.float32) + finished[rows_local:]).astype(jnp.bfloat16)

    return (
        block_output.reshape(1, rows_local, width),
        input_grad.reshape(1, rows_local, width),
        w_in_grad,
        w_out_grad,
    )


def solution(mesh):
    placed = (
        P("rep", "col", "row"),
        P("row", ("rep", "col")),
        P(("rep", "col"), "row"),
        P("rep", "col", "row"),
        P(),
    )
    return jax.shard_map(
        body,
        mesh=mesh,
        in_specs=placed,
        out_specs=(
            P("rep", "col", "row"),
            P("rep", "col", "row"),
            P("row", ("rep", "col")),
            P(("rep", "col"), "row"),
        ),
        check_vma=False,
    )
```
